256 devices in a mesh: seq: 64 (over z, y, x_lo), ch: 4 (over x_hi, core).
Axes of the slice: x: 4 (x_hi: 2, x_lo: 2; x = x_hi * 2 + x_lo), y: 4, z: 8, core: 2. Of those that a mesh axis runs over, the one named last changes fastest.
Arguments:
- tokens: bfloat16 [16384, 4096], P('seq', 'ch'), may hold values from -6 to 6
- in_weight: bfloat16 [4096, 3, 2048], P('seq', None, 'ch'), may hold values from -0.09375 to 0.09375
- short_filter: float32 [3, 3, 2048], P(None, None, 'ch'), may hold values from -3 to 3
- long_filter: float32 [16384, 2048], P('seq', 'ch'), may hold values from -0.046875 to 0.046875
- skip_gain: float32 [2048], P('ch'), may hold values from -4 to 4
Outputs:
- mixed: bfloat16 [16384, 2048], P('seq', 'ch')
The draws below stay inside these ranges and needn't reach their ends.
All inputs are finite; a program needn't handle non-finite values.
Results may differ from the reference program's by a relative error of at most 0.0019.
Values may be sent and summed in bfloat16 or wider, within the bound.
A program may use at most 128 MiB of HBM per device.

```python
import jax
import jax.numpy as jnp
from jax import lax

D = 4096
C = 2048
SHORT = 3
SEQ_LEN = 16384


def block_levels(stream_key, dims, cuts, smallest, high):
    gain, own = 1.0, jax.random.fold_in(stream_key, 6)
    for position, blocks in cuts:
        steps = jnp.exp(jax.random.uniform(jax.random.fold_in(own, position), (blocks,), jnp.float32, smallest / len(cuts), high / len(cuts)))
        gain = gain * jnp.repeat(steps, dims[position] // blocks).reshape([-1 if axis == position else 1 for axis in range(len(dims))])
    return gain


def bell_draw(stream_key, dims, scale, reach, cuts=(), held_as=jnp.bfloat16):
    factor_of = block_levels(stream_key, dims, cuts, -0.22, 0.18) if cuts else 1.0
    result = jax.random.normal(stream_key, dims, jnp.float32) * scale * factor_of
    return jnp.minimum(jnp.maximum(result, -reach), reach).astype(held_as)


def setup_inputs(seed: int = 0) -> dict:
    arg_keys = jax.random.split(jax.random.key(seed), 6)
    tokens = bell_draw(arg_keys[0], (SEQ_LEN, D), 1.0, 6.0, ((0, 64), (1, 4)))
    in_weight = bell_draw(arg_keys[1], (D, 3, C), D ** -0.5, 0.09375, ((0, 64), (2, 4)))
    short_filter = bell_draw(arg_keys[2], (SHORT, 3, C), 0.6, 3.0, ((2, 4),), jnp.float32)
    long_filter = bell_draw(arg_keys[3], (SEQ_LEN, C), SEQ_LEN ** -0.5, 0.046875, ((0, 64), (1, 4)), jnp.float32)
    skip_gain = bell_draw(arg_keys[4], (C,), 1.0, 4.0, ((0, 4),), jnp.float32)
    return {"tokens": tokens, "in_weight": in_weight, "short_filter": short_filter, "long_filter": long_filter, "skip_gain": skip_gain}


def reference(tokens, in_weight, short_filter, long_filter, skip_gain):
    length = tokens.shape[0]
    groups = 8
    group_width = C // groups
    weights = in_weight.reshape(D, 3, groups, group_width).transpose(2, 0, 1, 3)
    taps_all = short_filter.reshape(SHORT, 3, groups, group_width).transpose(2, 0, 1, 3)
    kernels = long_filter.reshape(length, groups, group_width).transpose(1, 0, 2)
    skip_rows = skip_gain.reshape(groups, group_width)

    def one_group(operands):
        weight_group, taps_group, kernel_group, skip_group = operands
        projected = jnp.dot(tokens, weight_group.reshape(D, 3 * group_width), preferred_element_type=jnp.float32)
        projected = projected.reshape(length, 3, group_width)
        padded = jnp.pad(projected, ((SHORT - 1, 0), (0, 0), (0, 0)))
        short_conv = jnp.zeros_like(projected)
        for offset in range(SHORT):
            start_row = SHORT - 1 - offset
            short_conv = short_conv + taps_group[offset] * padded[start_row:start_row + length]
        gate_product = short_conv[:, 1] * short_conv[:, 2]
        spectrum = jnp.fft.fft(gate_product, n=2 * length, axis=0)
        response = jnp.fft.fft(kernel_group, n=2 * length, axis=0)
        convolved = jnp.real(jnp.fft.ifft(spectrum * response, axis=0))[:length]
        return (short_conv[:, 0] * (convolved + skip_group * gate_product)).astype(jnp.bfloat16)

    mixed_groups = lax.map(one_group, (weights, taps_all, kernels, skip_rows))
    return mixed_groups.transpose(1, 0, 2).reshape(length, C)
```

```python
import math

import jax
import jax.numpy as jnp
import ml_dtypes
import numpy as np
from jax import lax
from jax.experimental import pallas as pl
from jax.experimental.pallas import tpu as pltpu
from jax.sharding import PartitionSpec as P

MESH = pl.DeviceIdType.MESH
BF16, F32 = jnp.bfloat16, jnp.float32

NZ, NY, NX = 8, 4, 4
SEQ, CH = 64, 4
BLOCKS = NZ * NY
TOK = 256
POS = 2 * TOK
FEAT = 1024
HALO = 16
TAPS = 3
WIDTH = 256
COLS = 3 * WIDTH
OWN = 8
WROWS = 64
SPLIT = 48
SIDE = 128
LENGTH = SIDE * SIDE
LO, HI = pl.ds(0, COLS // 2), pl.ds(COLS // 2, COLS // 2)


def split_table(table):
    high = table.astype(ml_dtypes.bfloat16)
    low = (table - high.astype(np.float64)).astype(ml_dtypes.bfloat16)
    return high, low


def tables():
    slot = np.arange(SIDE)
    n1 = 4 * (slot % BLOCKS) + slot // BLOCKS
    k = np.arange(SIDE)
    outer = 2.0 * math.pi * ((np.outer(4 * k + 1, n1)) % 512) / 512.0
    first = np.concatenate([np.cos(outer), -np.sin(outer)], axis=0)
    last = np.concatenate([np.cos(outer).T, -np.sin(outer).T], axis=1) / LENGTH
    inner = 2.0 * math.pi * (np.outer(k, k) % SIDE) / SIDE
    cos, sin = np.cos(inner), np.sin(inner)
    ahead = np.block([[cos, -sin], [sin, cos]])
    back = np.block([[cos, sin], [-sin, cos]])
    twist = 2.0 * math.pi * np.outer(4 * k + 1, k) / (4.0 * LENGTH)
    fh, fl = split_table(first)
    lh, ll = split_table(last)
    return (
        np.concatenate([fh, fh, fl], axis=1),
        np.concatenate([lh, lh, ll], axis=1),
        np.stack(split_table(ahead)),
        np.stack(split_table(back)),
        np.stack([np.cos(twist), np.sin(twist)]).astype(np.float32),
    )


def halves(values):
    high = values.astype(BF16)
    return high, (values - high.astype(F32)).astype(BF16)


def mm(a, b):
    return jnp.dot(a, b, preferred_element_type=F32)


def right_apply(values, table):
    high, low = halves(values)
    return mm(high, table[0]) + mm(low, table[0]) + mm(high, table[1])


def kernel(
    tokens, weights, filt, taps, skip, first, last, ahead, back, twist,
    out,
    w, tok, acc, filt_t, filt_in, gate_t, gate_in, outer_t, outer, y_out, y_in, spec,
    send, recv, many,
):
    seq = lax.axis_index("seq")
    ch = lax.axis_index("ch")
    x_lo, blk = seq % 2, seq // 2
    y, z = blk % NY, blk // NY
    x_hi, core = ch // 2, ch % 2
    x = x_hi * 2 + x_lo

    def seq_of(zz, yy, xx):
        return (zz * NY + yy) * 2 + xx

    def at_yz(dy, dz):
        return {"seq": seq_of((z + dz + NZ) % NZ, (y + dy + NY) % NY, x_lo)}

    def at_x(dx):
        xx = (x + dx + NX) % NX
        return {"seq": seq_of(z, y, xx % 2), "ch": (xx // 2) * 2 + core}

    twin = {"ch": x_hi * 2 + 1 - core}
    mate = {"seq": seq_of(z, y, 1 - x_lo)}

    barrier = pltpu.get_barrier_semaphore()

    def greet(i, _):
        pl.semaphore_signal(barrier, inc=1, device_id={"seq": (seq + i) % SEQ}, device_id_type=MESH)
        return 0

    lax.fori_loop(1, SEQ, greet, 0)
    pl.semaphore_signal(barrier, inc=1, device_id=twin, device_id_type=MESH)
    pl.semaphore_signal(barrier, inc=1, device_id=at_x(3 + 2 * x_lo), device_id_type=MESH)

    started = []
    slots = {}

    def slot(name):
        return slots.setdefault(name, len(slots))

    def go(name, src, dst, device):
        copy = pltpu.make_async_remote_copy(
            src_ref=src, dst_ref=dst, send_sem=send.at[slot(name)], recv_sem=recv.at[slot(name)],
            device_id=device, device_id_type=MESH,
        )
        copy.start()
        started.append(copy)

    def arrived(name, dst):
        pltpu.make_async_copy(dst, dst, recv.at[slot(name)]).wait()

    def local(name, src, dst):
        copy = pltpu.make_async_copy(src, dst, recv.at[slot(name)])
        copy.start()
        return copy

    def block(dy, dz):
        return ((z - dz + NZ) % NZ) * NY + (y - dy + NY) % NY

    def yf(dy, lanes=slice(None)):
        return w.at[block(dy, 0), pl.ds(0, SPLIT), lanes]

    def yf_plane(dz, lanes=slice(None)):
        return w.at[pl.ds(((z - dz + NZ) % NZ) * NY, NY), pl.ds(0, SPLIT), lanes]

    def zf(dy, dz, lanes=slice(None)):
        return w.at[block(dy, dz), pl.ds(SPLIT, 2 * WROWS - SPLIT), lanes]

    def tk(dx, cc, start=0, rows=TOK):
        xx = (x - dx + NX) % NX
        row = pl.multiple_of(HALO + (xx % 2) * TOK + start, 16)
        col = pl.multiple_of(((xx // 2) * 2 + cc) * FEAT, FEAT)
        return tok.at[pl.ds(row, rows), pl.ds(col, FEAT)]

    HALF = TOK // 2

    own_w = local("own_w", weights.at[x_lo], w.at[blk, pl.ds(pl.multiple_of(x_lo * WROWS, WROWS), WROWS)])
    own_tok = local("own_tok", tokens, tk(0, core))
    for i in range(4):
        for j in range(2):
            filt_t[j, i * 128 : (i + 1) * 128, :] = filt[
                j * 128 : (j + 1) * 128, i * 128 : (i + 1) * 128
            ].T
    pl.semaphore_wait(barrier, SEQ + 1)

    other_rows = w.at[blk, pl.ds(pl.multiple_of((1 - x_lo) * WROWS, WROWS), WROWS)]
    go("swap", weights.at[1 - x_lo], w.at[blk, pl.ds(pl.multiple_of(x_lo * WROWS, WROWS), WROWS)], mate)
    go("tok+1", tokens, tk(0, core), at_x(1))
    go("tok-1", tokens, tk(0, core), at_x(-1))
    go("core0", tokens, tk(0, core), twin)

    own_w.wait()
    arrived("swap", other_rows)

    def send_zfy(dz):
        go(f"zfy{dz},+1", zf(0, dz), zf(0, dz), at_yz(1, 0))
        go(f"zfy{dz},-1", zf(0, dz), zf(0, dz), at_yz(-1, 0))

    def pass_zfy(dz):
        arrived(f"zfy{dz},+1", zf(1, dz))
        go(f"zfy{dz},+2", zf(1, dz, LO), zf(1, dz, LO), at_yz(1, 0))
        arrived(f"zfy{dz},-1", zf(-1, dz))
        go(f"zfy{dz},-2", zf(-1, dz, HI), zf(-1, dz, HI), at_yz(-1, 0))

    def end_zfy(dz):
        arrived(f"zfy{dz},+2", zf(2, dz, LO))
        arrived(f"zfy{dz},-2", zf(-2, dz, HI))

    def send_zf(dz):
        far = dz == 3
        for sign, lanes in ((1, LO), (-1, HI)):
            lanes = lanes if far else slice(None)
            ref = zf(0, sign * dz, lanes)
            go(f"zf{sign * (dz + 1)}", ref, ref, at_yz(0, sign))

    def end_zf(dz):
        for sign, lanes in ((1, LO), (-1, HI)):
            arrived(f"zf{sign * dz}", zf(0, sign * dz, lanes if dz == 4 else slice(None)))

    def send_plane(dz):
        far = dz == 3
        for sign, lanes in ((1, LO), (-1, HI)):
            lanes = lanes if far else slice(None)
            ref = yf_plane(sign * dz, lanes)
            go(f"plane{sign * (dz + 1)}", ref, ref, at_yz(0, sign))

    def end_plane(dz):
        for sign, lanes in ((1, LO), (-1, HI)):
            arrived(f"plane{sign * dz}", yf_plane(sign * dz, lanes if dz == 4 else slice(None)))

    def project(dz, fresh=False):
        plane = (z - dz + NZ) % NZ

        def part(i, _):
            cols = pl.ds(pl.multiple_of(i * 256, 256), 256)
            term = mm(
                tok[:, pl.ds(pl.multiple_of(plane * 512, 512), 512)],
                w[pl.ds(plane * NY, NY), :, cols].reshape(512, 256),
            )
            acc[:, cols] = term if fresh else acc[:, cols] + term
            return 0

        lax.fori_loop(0, 3, part, 0)

    go("yf+1", yf(0), yf(0), at_yz(1, 0))
    go("yf-1", yf(0), yf(0), at_yz(-1, 0))
    send_zf(0)
    send_zfy(0)

    arrived("yf+1", yf(1))
    go("yf+2", yf(1, LO), yf(1, LO), at_yz(1, 0))
    arrived("yf-1", yf(-1))
    go("yf-2", yf(-1, HI), yf(-1, HI), at_yz(-1, 0))

    end_zf(1)
    send_zf(1)
    send_zfy(1)
    send_zfy(-1)

    arrived("yf+2", yf(2, LO))
    arrived("yf-2", yf(-2, HI))
    send_plane(0)

    def give_filter(i, _):
        peer = (seq + i) % SEQ
        pltpu.make_async_remote_copy(
            src_ref=filt_t.at[:, pl.ds(pl.multiple_of((peer % 2) * WIDTH + (peer // 2) * OWN, OWN), OWN)],
            dst_ref=filt_in.at[:, pl.ds(pl.multiple_of(seq * OWN, OWN), OWN)],
            send_sem=many.at[0], recv_sem=many.at[1], device_id={"seq": peer}, device_id_type=MESH,
        ).start()
        return 0

    lax.fori_loop(1, SEQ, give_filter, 0)
    pltpu.make_async_copy(
        filt_t.at[:, pl.ds(pl.multiple_of(x_lo * WIDTH + blk * OWN, OWN), OWN)],
        filt_in.at[:, pl.ds(pl.multiple_of(seq * OWN, OWN), OWN)],
        many.at[1],
    ).start()

    pass_zfy(0)
    end_zf(2)
    send_zf(2)
    send_zfy(2)
    send_zfy(-2)
    end_zf(3)
    send_zf(3)
    send_zfy(3)
    send_zfy(-3)
    pass_zfy(1)
    pass_zfy(-1)
    end_zf(4)
    send_zfy(4)

    arrived("tok+1", tk(1, core))
    go("tok+2", tk(1, core, 0, HALF), tk(1, core, 0, HALF), at_x(1))
    go("core+1", tk(1, core), tk(1, core), twin)
    arrived("tok-1", tk(-1, core))
    go("tok-2", tk(-1, core, HALF, HALF), tk(-1, core, HALF, HALF), at_x(-1))
    go("core-1", tk(-1, core), tk(-1, core), twin)

    end_plane(1)
    send_plane(1)
    pass_zfy(2)
    pass_zfy(-2)

    arrived("tok+2", tk(2, core, 0, HALF))
    go("core+2", tk(2, core, 0, HALF), tk(2, core, 0, HALF), twin)
    arrived("tok-2", tk(2, core, HALF, HALF))
    go("core-2", tk(2, core, HALF, HALF), tk(2, core, HALF, HALF), twin)
    own_tok.wait()
    arrived("core0", tk(0, 1 - core))
    arrived("core+1", tk(1, 1 - core))
    arrived("core-1", tk(-1, 1 - core))
    arrived("core+2", tk(2, 1 - core, 0, HALF))
    arrived("core-2", tk(2, 1 - core, HALF, HALF))
    after = (blk + 1) % BLOCKS
    go("halo", tok.at[pl.ds(POS, HALO)], tok.at[pl.ds(0, HALO)], {"seq": after * 2 + x_lo})

    end_zfy(0)
    pass_zfy(3)
    pass_zfy(-3)
    end_plane(2)
    send_plane(2)
    arrived("halo", tok.at[pl.ds(0, HALO)])
    project(0, fresh=True)
    end_zfy(1)
    end_zfy(-1)
    project(1)
    project(-1)
    pass_zfy(4)
    end_plane(3)
    send_plane(3)

    def transform(load, pair):
        columns = jnp.concatenate([load(2 * pair), load(2 * pair + 1)], axis=1)
        high, low = halves(columns)
        turned = mm(first[...], jnp.concatenate([high, low, high], axis=0))
        cos, sin = twist[0], twist[1]
        rows = []
        for i in range(2):
            real = turned[:SIDE, i * SIDE : (i + 1) * SIDE]
            imag = turned[SIDE:, i * SIDE : (i + 1) * SIDE]
            rows.append(jnp.concatenate([real * cos + imag * sin, imag * cos - real * sin], axis=1))
        return right_apply(jnp.concatenate(rows, axis=0), ahead)

    def load_filter(c):
        return jnp.concatenate(
            [
                filt_in[j % 2, pl.ds(c + OWN * (j // 2), BLOCKS, stride=2 * OWN), :]
                for j in range(4)
            ],
            axis=0,
        )

    def load_gate(c):
        return jnp.concatenate(
            [gate_in[j, pl.ds(c, BLOCKS, stride=OWN), :] for j in range(4)], axis=0
        )

    pltpu.make_async_copy(filt_in, filt_in, many.at[1]).wait()
    for pair in range(OWN // 2):
        spec[pair * 256 : (pair + 1) * 256, :] = transform(load_filter, pair)

    end_zfy(2)
    end_zfy(-2)
    project(2)
    project(-2)
    end_zfy(3)
    end_zfy(-3)
    project(3)
    project(-3)
    end_plane(4)
    end_zfy(4)
    project(4)

    acc[8:16, :] = jnp.where(blk == 0, 0.0, acc[8:16, :])
    taps_col = pl.ds(pl.multiple_of(x_lo * WIDTH, WIDTH), WIDTH)
    tap = [[taps[pl.ds(3 * j + s, 1), taps_col] for s in range(3)] for j in range(TAPS)]
    for lane in range(2):
        for row in range(4):

            def short(s):
                total = None
                for j in range(TAPS):
                    cols = slice(s * WIDTH + lane * 128, s * WIDTH + (lane + 1) * 128)
                    start = HALO - j + row * 128
                    term = tap[j][s][:, lane * 128 : (lane + 1) * 128] * acc[start : start + 128, cols]
                    total = term if total is None else total + term
                return total

            place = (row, slice(lane * 128, (lane + 1) * 128))
            gate_t[place] = (short(1) * short(2)).T
            outer_t[place] = short(0).T

    def give_gate(i, _):
        peer = (blk + i) % BLOCKS
        pltpu.make_async_remote_copy(
            src_ref=gate_t.at[:, pl.ds(pl.multiple_of(peer * OWN, OWN), OWN)],
            dst_ref=gate_in.at[:, pl.ds(pl.multiple_of(blk * OWN, OWN), OWN)],
            send_sem=many.at[2], recv_sem=many.at[3], device_id={"seq": peer * 2 + x_lo}, device_id_type=MESH,
        ).start()
        return 0

    lax.fori_loop(1, BLOCKS, give_gate, 0)
    pltpu.make_async_copy(
        gate_t.at[:, pl.ds(pl.multiple_of(blk * OWN, OWN), OWN)],
        gate_in.at[:, pl.ds(pl.multiple_of(blk * OWN, OWN), OWN)],
        many.at[3],
    ).start()
    mine = pl.ds(pl.multiple_of(x_lo * WIDTH, WIDTH), WIDTH)
    theirs = pl.ds(pl.multiple_of((1 - x_lo) * WIDTH, WIDTH), WIDTH)
    go("outer", outer_t.at[pl.ds(2 * (1 - x_lo), 2)], outer.at[:, mine], mate)
    own_outer = local("own_outer", outer_t.at[pl.ds(2 * x_lo, 2)], outer.at[:, mine])
    pltpu.make_async_copy(gate_in, gate_in, many.at[3]).wait()

    for pair in range(OWN // 2):
        spectrum = transform(load_gate, pair)
        response = spec[pair * 256 : (pair + 1) * 256, :]
        sr, si = spectrum[:, :SIDE], spectrum[:, SIDE:]
        rr, ri = response[:, :SIDE], response[:, SIDE:]
        product = jnp.concatenate([sr * rr - si * ri, sr * ri + si * rr], axis=1)
        inverse = right_apply(product, back)
        cos, sin = twist[0], twist[1]
        cols = []
        for i in range(2):
            real = inverse[i * SIDE : (i + 1) * SIDE, :SIDE]
            imag = inverse[i * SIDE : (i + 1) * SIDE, SIDE:]
            cols.append(jnp.concatenate([real * cos - imag * sin, imag * cos + real * sin], axis=0))
        high, low = halves(jnp.concatenate(cols, axis=1))
        result = mm(last[...], jnp.concatenate([high, low, high], axis=0))
        for i in range(2):
            c = 2 * pair + i
            gain = skip[x_lo * WIDTH + blk * OWN + c]
            total = result[:, i * SIDE : (i + 1) * SIDE] + gain * load_gate(c)
            for j in range(4):
                y_out[j, pl.ds(c, BLOCKS, stride=OWN), :] = total[j * BLOCKS : (j + 1) * BLOCKS, :]

    rows_here = pl.ds(pl.multiple_of(x_lo * WIDTH + blk * OWN, OWN), OWN)

    def chunk(peer):
        return y_out.at[pl.ds((peer % 2) * 2, 2), pl.ds(pl.multiple_of((peer // 2) * OWN, OWN), OWN)]

    def give_y(i, _):
        peer = (seq + i) % SEQ
        pltpu.make_async_remote_copy(
            src_ref=chunk(peer), dst_ref=y_in.at[:, rows_here],
            send_sem=many.at[4], recv_sem=many.at[5], device_id={"seq": peer}, device_id_type=MESH,
        ).start()
        return 0

    lax.fori_loop(1, SEQ, give_y, 0)
    pltpu.make_async_copy(chunk(seq), y_in.at[:, rows_here], many.at[5]).start()
    own_outer.wait()
    arrived("outer", outer.at[:, theirs])
    pltpu.make_async_copy(y_in, y_in, many.at[5]).wait()
    for i in range(4):
        for j in range(2):
            place = (j, slice(i * 128, (i + 1) * 128))
            out[j * 128 : (j + 1) * 128, i * 128 : (i + 1) * 128] = (outer[place] * y_in[place]).T

    for copy in started:
        copy.wait_send()
    sent = filt_t.at[:, pl.ds(OWN, (SEQ - 1) * OWN)]
    pltpu.make_async_copy(sent, sent, many.at[0]).wait()
    sent = gate_t.at[:, pl.ds(OWN, (BLOCKS - 1) * OWN)]
    pltpu.make_async_copy(sent, sent, many.at[2]).wait()
    sent = y_in.at[:, pl.ds(OWN, (SEQ - 1) * OWN)]
    pltpu.make_async_copy(sent, sent, many.at[4]).wait()


SLOTS = 80


def local(tokens, in_weight, short_filter, long_filter, skip_gain):
    width = skip_gain.shape[0]
    weights = in_weight.reshape(WROWS, 3, 2, WIDTH).transpose(2, 0, 1, 3).reshape(2, WROWS, COLS)
    taps = short_filter.reshape(3 * TAPS, width)
    vmem = pl.BlockSpec(memory_space=pltpu.VMEM)
    anywhere = pl.BlockSpec(memory_space=pl.ANY)
    out = pl.pallas_call(
        kernel,
        out_shape=jax.ShapeDtypeStruct((TOK, width), F32),
        in_specs=[anywhere, anywhere, vmem, vmem, pl.BlockSpec(memory_space=pltpu.SMEM)] + [vmem] * 5,
        out_specs=vmem,
        scratch_shapes=[
            pltpu.VMEM((BLOCKS, 2 * WROWS, COLS), BF16),
            pltpu.VMEM((HALO + POS, CH * FEAT), BF16),
            pltpu.VMEM((HALO + POS, COLS), F32),
            pltpu.VMEM((2, 2 * WIDTH, SIDE), F32),
            pltpu.VMEM((2, 2 * WIDTH, SIDE), F32),
            pltpu.VMEM((4, WIDTH, SIDE), F32),
            pltpu.VMEM((4, WIDTH, SIDE), F32),
            pltpu.VMEM((4, WIDTH, SIDE), F32),
            pltpu.VMEM((2, 2 * WIDTH, SIDE), F32),
            pltpu.VMEM((4, WIDTH, SIDE), F32),
            pltpu.VMEM((2, 2 * WIDTH, SIDE), F32),
            pltpu.VMEM((OWN * SIDE, 2 * SIDE), F32),
            pltpu.SemaphoreType.DMA((SLOTS,)),
            pltpu.SemaphoreType.DMA((SLOTS,)),
            pltpu.SemaphoreType.DMA((6,)),
        ],
        compiler_params=pltpu.CompilerParams(
            collective_id=0, has_side_effects=True, vmem_limit_bytes=40 * 1024 * 1024
        ),
    )(tokens, weights, long_filter, taps, skip_gain, *tables())
    return out.astype(BF16)


def solution(mesh):
    placed = (P("seq", "ch"), P("seq", None, "ch"), P(None, None, "ch"), P("seq", "ch"), P("ch"))
    return jax.shard_map(
        local, mesh=mesh, in_specs=placed, out_specs=P("seq", "ch"), check_vma=False
    )
```

```python
import math

import jax
import jax.numpy as jnp
import ml_dtypes
import numpy as np
from jax import lax
from jax.experimental import pallas as pl
from jax.experimental.pallas import tpu as pltpu
from jax.sharding import PartitionSpec as P

MESH = pl.DeviceIdType.MESH
BF16, F32 = jnp.bfloat16, jnp.float32

NZ, NY, NX = 8, 4, 4
AROUND = (1, -1, 2, -2)
SEQ, CH = 64, 4
BLOCKS = NZ * NY
TOK = 256
POS = 2 * TOK
FEAT = 1024
HALO = 16
TAPS = 3
WIDTH = 256
COLS = 3 * WIDTH
OWN = 8
WROWS = 64
SPLIT = 48
SIDE = 128
LENGTH = SIDE * SIDE
SPREAD = 27
LO, HI = pl.ds(0, WIDTH // 2), pl.ds(WIDTH // 2, WIDTH // 2)
REST = 2 * WROWS - SPLIT


SWAP, ZF_OWN, ZF_ADDED, ZF, ZFY_OWN, ZFY_ADDED, ZFY, YF, PLANE, TOKEN, CORE, LAST_ROWS, TURN, GIVE, RESPOND, PROJECT = range(16)


def key(kind, first=0, second=0):
    return 100 * kind + 10 * (first + 4) + second + 4


STEPS = (
    44, 454, 434, 134, 154, 1244, 1044, 954, 934, 1304, 1314, 534, 554, 254, 734, 754, 234, 1324, 642, 646, 655,
    653, 364, 633, 635, 324, 1334, 724, 764, 1344, 1354, 1054, 964, 856, 834, 835, 836, 857, 855, 837, 854, 1034,
    924, 1364, 665, 663, 625, 623, 314, 374, 652, 656, 632, 636, 1064, 1024, 1144, 866, 824, 825, 826, 867, 865,
    827, 864, 1444, 662, 626, 622, 666, 615, 613, 304, 675, 673, 384, 1544, 1554, 1534, 876, 814, 815, 877, 875,
    817, 874, 816, 1564, 685, 683, 1524, 612, 672, 616, 676, 886, 804, 805, 887, 885, 884, 806, 807, 682, 686, 1514,
    1574, 1584,
)


def split_table(table):
    high = table.astype(ml_dtypes.bfloat16)
    low = (table - high.astype(np.float64)).astype(ml_dtypes.bfloat16)
    return high, low


def tables():
    slot = np.arange(SIDE)
    n1 = 4 * (slot % BLOCKS) + slot // BLOCKS
    k = np.arange(SIDE)
    outer = 2.0 * math.pi * ((np.outer(4 * k + 1, n1)) % 512) / 512.0
    first = np.concatenate([np.cos(outer), -np.sin(outer)], axis=0)
    last = np.concatenate([np.cos(outer).T, -np.sin(outer).T], axis=1) / LENGTH
    inner = 2.0 * math.pi * (np.outer(k, k) % SIDE) / SIDE
    cos, sin = np.cos(inner), np.sin(inner)
    ahead = np.block([[cos, -sin], [sin, cos]])
    back = np.block([[cos, sin], [-sin, cos]])
    twist = 2.0 * math.pi * np.outer(4 * k + 1, k) / (4.0 * LENGTH)
    fh, fl = split_table(first)
    lh, ll = split_table(last)
    return (
        np.concatenate([fh, fh, fl], axis=1),
        np.concatenate([lh, lh, ll], axis=1),
        np.stack(split_table(ahead)),
        np.stack(split_table(back)),
        np.stack([np.cos(twist), np.sin(twist)]).astype(np.float32),
    )


def halves(values):
    high = values.astype(BF16)
    return high, (values - high.astype(F32)).astype(BF16)


def mm(a, b):
    return jnp.dot(a, b, preferred_element_type=F32)


def right_apply(values, table):
    high, low = halves(values)
    return mm(high, table[0]) + mm(low, table[0]) + mm(high, table[1])


def kernel(
    tokens, weights, filt_hbm, taps_hbm, skip_hbm, first_hbm, last_hbm, ahead_hbm, back_hbm, twist_hbm,
    out,
    filt, taps, skip, first, last, ahead, back, twist,
    w, tok, acc, filt_t, filt_in, gate_t, gate_in, outer_t, outer, y_out, y_in, spec,
    send, recv, many,
):
    seq = lax.axis_index("seq")
    ch = lax.axis_index("ch")
    x_lo, blk = seq % 2, seq // 2
    y, z = blk % NY, blk // NY
    x_hi, core = ch // 2, ch % 2
    x = x_hi * 2 + x_lo

    def seq_of(zz, yy, xx):
        return (zz * NY + yy) * 2 + xx

    def at_yz(dy, dz):
        return {"seq": seq_of((z + dz + NZ) % NZ, (y + dy + NY) % NY, x_lo)}

    def at_x(dx):
        xx = (x + dx + NX) % NX
        return {"seq": seq_of(z, y, xx % 2), "ch": (xx // 2) * 2 + core}

    twin = {"ch": x_hi * 2 + 1 - core}
    mate = {"seq": seq_of(z, y, 1 - x_lo)}

    started = []
    slots = {}

    def slot(name):
        return slots.setdefault(name, len(slots))

    def go(name, src, dst, device):
        copy = pltpu.make_async_remote_copy(
            src_ref=src, dst_ref=dst, send_sem=send.at[slot(name)], recv_sem=recv.at[slot(name)],
            device_id=device, device_id_type=MESH,
        )
        copy.start()
        started.append(copy)

    def arrived(name, dst):
        pltpu.make_async_copy(dst, dst, recv.at[slot(name)]).wait()

    def local(name, src, dst):
        copy = pltpu.make_async_copy(src, dst, recv.at[slot(name)])
        copy.start()
        return copy

    def block(dy, dz):
        return ((z - dz + NZ) % NZ) * NY + (y - dy + NY) % NY

    early = pl.multiple_of(x_lo * SPLIT, 16)
    late = pl.multiple_of((1 - x_lo) * REST, 16)
    own_rows = pl.ds(pl.multiple_of(x_lo * WROWS, WROWS), WROWS)
    mate_rows = pl.ds(pl.multiple_of((1 - x_lo) * WROWS, WROWS), WROWS)
    added_rows = pl.ds(pl.multiple_of(x_lo * SPLIT + (1 - x_lo) * WROWS, 16), REST - WROWS)

    def yf(dy, lanes=slice(None)):
        return w.at[block(dy, 0), :, pl.ds(late, SPLIT), lanes]

    def yf_plane(dz, piece, lanes=slice(None)):
        return w.at[((z - dz + NZ) % NZ) * NY + piece, :, pl.ds(late, SPLIT), lanes]

    def zf(dy, dz, lanes=slice(None), rows=pl.ds(early, REST)):
        return w.at[block(dy, dz), :, rows, lanes]

    def tk(dx, cc, start=0, rows=TOK):
        xx = (x - dx + NX) % NX
        row = pl.multiple_of(HALO + (xx % 2) * TOK + start, 16)
        col = pl.multiple_of(((xx // 2) * 2 + cc) * FEAT, FEAT)
        return tok.at[pl.ds(row, rows), pl.ds(col, FEAT)]

    HALF = TOK // 2

    mine = pl.ds(pl.multiple_of(x_lo * WIDTH, WIDTH), WIDTH)
    theirs = pl.ds(pl.multiple_of((1 - x_lo) * WIDTH, WIDTH), WIDTH)
    own_w = local(-1, weights.at[:, :, mine], w.at[blk, :, own_rows])
    own_filt = local(-2, filt_hbm, filt)
    own_tok = local(-3, tokens, tk(0, core))
    tables_in = [
        local(name, src, dst)
        for name, src, dst in (
            (-5, first_hbm, first), (-6, last_hbm, last), (-7, ahead_hbm, ahead), (-8, back_hbm, back),
            (-9, twist_hbm, twist), (-10, taps_hbm, taps), (-11, skip_hbm, skip),
        )
    ]

    barrier = pltpu.get_barrier_semaphore()

    def greet(i, _):
        pl.semaphore_signal(barrier, inc=1, device_id={"seq": (seq + i) % SEQ}, device_id_type=MESH)
        return 0

    lax.fori_loop(1, SEQ, greet, 0)
    pl.semaphore_signal(barrier, inc=1, device_id=twin, device_id_type=MESH)
    pl.semaphore_signal(barrier, inc=1, device_id=at_x(3 + 2 * x_lo), device_id_type=MESH)
    pl.semaphore_wait(barrier, SEQ + 1)

    own_w.wait()

    copies = {}

    def plan(name, src, device, after, comes, dst=None):
        copies[name] = (src, src if dst is None else dst, device, after, comes)

    def zf_parts(dz):
        if dz == 0:
            return [key(SWAP)]
        if abs(dz) == 1:
            return [key(ZF_OWN, dz), key(ZF_ADDED, dz)]
        return [key(ZF, 4), key(ZF, -4)] if dz == 4 else [key(ZF, dz)]

    everything = slice(None)
    plan(key(SWAP), weights.at[:, :, theirs], mate, [], w.at[blk, :, mate_rows], w.at[blk, :, own_rows])
    for sign, lanes in ((1, LO), (-1, HI)):
        for own, own_y, rows, after in (
            (ZF_OWN, ZFY_OWN, own_rows, []), (ZF_ADDED, ZFY_ADDED, added_rows, [key(SWAP)]),
        ):
            ref = zf(0, 0, rows=rows)
            plan(key(own, sign), ref, at_yz(0, sign), after, zf(0, sign, rows=rows))
            plan(key(own_y, sign), ref, at_yz(sign, 0), after, zf(sign, 0, rows=rows))
        for dz in (2, 3, 4):
            part = lanes if dz == 4 else everything
            far = sign * dz
            plan(key(ZF, far), zf(0, far - sign, part), at_yz(0, sign), zf_parts(far - sign), zf(0, far, part))
        for dz in range(-3, 5):
            after = [key(ZFY_OWN, sign), key(ZFY_ADDED, sign)]
            if dz != 0:
                after = [key(ZFY, dz, sign)]
                plan(after[0], zf(0, dz), at_yz(sign, 0), zf_parts(dz), zf(sign, dz))
            plan(key(ZFY, dz, 2 * sign), zf(sign, dz, lanes), at_yz(sign, 0), after, zf(2 * sign, dz, lanes))
        plan(key(YF, sign), yf(0), at_yz(sign, 0), [key(SWAP)], yf(sign))
        plan(key(YF, 2 * sign), yf(sign, lanes), at_yz(sign, 0), [key(YF, sign)], yf(2 * sign, lanes))
        for dz in (1, 2, 3, 4):
            part = lanes if dz == 4 else everything
            for piece in range(NY):
                near = sign * (dz - 1)
                after = [key(PLANE, near, piece)] if dz > 1 else [key(YF, by) for by in AROUND]
                plan(
                    key(PLANE, sign * dz, piece), yf_plane(near, piece, part), at_yz(0, sign), after,
                    yf_plane(sign * dz, piece, part),
                )
        start = 0 if sign == 1 else HALF
        plan(key(TOKEN, sign), tokens, at_x(sign), [], tk(sign, core), tk(0, core))
        plan(
            key(TOKEN, 2 * sign), tk(sign, core, start, HALF), at_x(sign), [key(TOKEN, sign)],
            tk(2, core, start, HALF),
        )
        plan(key(CORE, sign), tk(sign, core), twin, [key(TOKEN, sign)], tk(sign, 1 - core))
        plan(
            key(CORE, 2 * sign), tk(2, core, start, HALF), twin, [key(TOKEN, 2 * sign)],
            tk(2, 1 - core, start, HALF),
        )
    plan(key(CORE), tokens, twin, [], tk(0, 1 - core), tk(0, core))
    after = (blk + 1) % BLOCKS
    all_tok = [key(kind, by) for kind in (TOKEN, CORE) for by in AROUND] + [key(CORE)]
    halo = tok.at[pl.ds(0, HALO)]
    plan(key(LAST_ROWS), tok.at[pl.ds(POS, HALO)], {"seq": after * 2 + x_lo}, all_tok, halo, halo)

    here = set()

    def need(names):
        for name in names:
            if name not in here:
                arrived(name, copies[name][4])
                here.add(name)

    def plane_parts(dz):
        parts = zf_parts(dz) + [key(ZFY, dz, by) for by in (2, -2)]
        if dz == 0:
            near = [key(kind, by) for kind in (ZFY_OWN, ZFY_ADDED) for by in (1, -1)]
            return parts + near + [key(YF, by) for by in AROUND]
        ends = (4, -4) if dz == 4 else (dz,)
        parts += [key(ZFY, dz, by) for by in (1, -1)]
        return parts + [key(PLANE, end, piece) for end in ends for piece in range(NY)]

    def project(dz, fresh=False):
        plane = (z - dz + NZ) % NZ

        def part(i, _):
            cols = pl.ds(pl.multiple_of(i * 256, 256), 256)
            term = mm(
                tok[:, pl.ds(pl.multiple_of(plane * 512, 512), 512)],
                w[pl.ds(plane * NY, NY), i].reshape(512, 256),
            )
            acc[:, cols] = term if fresh else acc[:, cols] + term
            return 0

        lax.fori_loop(0, 3, part, 0)

    def rows8(index):
        return pl.ds(pl.multiple_of(index * 8, 8), 8)

    def rows16(index):
        return pl.ds(pl.multiple_of(index * 16, 16), 16)

    def turn_filter():
        own_filt.wait()
        for i in range(4):
            for j in range(2):
                filt_t[i % 2, pl.ds((i // 2) * WIDTH + j, SIDE, stride=2), :] = filt[
                    j * 128 : (j + 1) * 128, i * 128 : (i + 1) * 128
                ].T
        pltpu.make_async_copy(filt_t.at[:, rows8(x_lo * BLOCKS + blk)], filt_in.at[:, rows8(seq)], many.at[1]).start()

    def give_filter(part):
        def give(i, _):
            peer = (seq + SPREAD * i) % SEQ
            pltpu.make_async_remote_copy(
                src_ref=filt_t.at[:, rows8((peer % 2) * BLOCKS + peer // 2)], dst_ref=filt_in.at[:, rows8(seq)],
                send_sem=many.at[0], recv_sem=many.at[1], device_id={"seq": peer}, device_id_type=MESH,
            ).start()
            return 0

        lax.fori_loop(1 + 9 * part, 10 + 9 * part, give, 0)

    def transform(load, pair):
        columns = jnp.concatenate([load(2 * pair), load(2 * pair + 1)], axis=1)
        high, low = halves(columns)
        turned = mm(first[...], jnp.concatenate([high, low, high], axis=0))
        cos, sin = twist[0], twist[1]
        rows = []
        for i in range(2):
            real = turned[:SIDE, i * SIDE : (i + 1) * SIDE]
            imag = turned[SIDE:, i * SIDE : (i + 1) * SIDE]
            rows.append(jnp.concatenate([real * cos + imag * sin, imag * cos - real * sin], axis=1))
        return right_apply(jnp.concatenate(rows, axis=0), ahead)

    def load_filter(c):
        return jnp.concatenate(
            [
                filt_in[c // 4, pl.ds(8 * (j // 2) + 2 * (c % 4) + j % 2, BLOCKS, stride=16), :]
                for j in range(4)
            ],
            axis=0,
        )

    def load_gate(c):
        return jnp.concatenate(
            [gate_in[c // 4, pl.ds(4 * (c % 4) + j, BLOCKS, stride=16), :] for j in range(4)], axis=0
        )

    def respond():
        for copy in tables_in:
            copy.wait()
        pltpu.make_async_copy(filt_in, filt_in, many.at[1]).wait()
        for pair in range(OWN // 2):
            spec[pair * 256 : (pair + 1) * 256, :] = transform(load_filter, pair)

    fresh = True
    for step in STEPS:
        kind, number = step // 100, step // 10 % 10 - 4
        if step in copies:
            src, dst, device, after, _ = copies[step]
            need(after)
            if kind == LAST_ROWS:
                own_tok.wait()
            go(step, src, dst, device)
        elif kind == PROJECT:
            need([key(LAST_ROWS)] if fresh else [])
            need(plane_parts(number))
            project(number, fresh)
            fresh = False
        elif kind == GIVE:
            give_filter(number + 4)
        elif kind == TURN:
            turn_filter()
        else:
            respond()
    assert here == set(copies)

    acc[8:16, :] = jnp.where(blk == 0, 0.0, acc[8:16, :])
    taps_col = pl.ds(pl.multiple_of(x_lo * WIDTH, WIDTH), WIDTH)
    tap = [[taps[j, pl.ds(s, 1), taps_col] for s in range(3)] for j in range(TAPS)]

    def give_gate(half):
        def give(i, _):
            peer = (blk + SPREAD * i) % BLOCKS
            pltpu.make_async_remote_copy(
                src_ref=gate_t.at[half, rows16(peer)], dst_ref=gate_in.at[half, rows16(blk)],
                send_sem=many.at[2], recv_sem=many.at[3 + half], device_id={"seq": peer * 2 + x_lo},
                device_id_type=MESH,
            ).start()
            return 0

        lax.fori_loop(1, BLOCKS, give, 0)
        pltpu.make_async_copy(gate_t.at[half, rows16(blk)], gate_in.at[half, rows16(blk)], many.at[3 + half]).start()

    for half in range(2):
        lanes = slice(half * SIDE, (half + 1) * SIDE)
        for row in range(4):

            def short(s):
                total = None
                for j in range(TAPS):
                    start = HALO - j + row * SIDE
                    cols = slice(s * WIDTH + half * SIDE, s * WIDTH + (half + 1) * SIDE)
                    term = tap[j][s][:, lanes] * acc[start : start + SIDE, cols]
                    total = term if total is None else total + term
                return total

            gate_t[half, pl.ds(row, SIDE, stride=4), :] = (short(1) * short(2)).T
            outer_t[row, lanes, :] = short(0).T
        give_gate(half)
    go(-4, outer_t.at[pl.ds(2 * (1 - x_lo), 2)], outer.at[:, mine], mate)
    own_outer = local(-12, outer_t.at[pl.ds(2 * x_lo, 2)], outer.at[:, mine])

    def convolve(pair):
        spectrum = transform(load_gate, pair)
        response = spec[pair * 256 : (pair + 1) * 256, :]
        sr, si = spectrum[:, :SIDE], spectrum[:, SIDE:]
        rr, ri = response[:, :SIDE], response[:, SIDE:]
        product = jnp.concatenate([sr * rr - si * ri, sr * ri + si * rr], axis=1)
        inverse = right_apply(product, back)
        cos, sin = twist[0], twist[1]
        cols = []
        for i in range(2):
            real = inverse[i * SIDE : (i + 1) * SIDE, :SIDE]
            imag = inverse[i * SIDE : (i + 1) * SIDE, SIDE:]
            cols.append(jnp.concatenate([real * cos - imag * sin, imag * cos + real * sin], axis=0))
        high, low = halves(jnp.concatenate(cols, axis=1))
        result = mm(last[...], jnp.concatenate([high, low, high], axis=0))
        for i in range(2):
            c = 2 * pair + i
            gain = skip[x_lo * WIDTH + (c // 4) * SIDE + blk * 4 + c % 4]
            total = result[:, i * SIDE : (i + 1) * SIDE] + gain * load_gate(c)
            for j in range(4):
                place = pl.ds(8 * (j // 2) + 2 * (c % 4) + j % 2, BLOCKS, stride=16)
                y_out[c // 4, place, :] = total[j * BLOCKS : (j + 1) * BLOCKS, :]

    def give_y(half):
        here8 = rows8(x_lo * BLOCKS + blk)

        def give(i, _):
            peer = (seq + SPREAD * i) % SEQ
            pltpu.make_async_remote_copy(
                src_ref=y_out.at[half, rows8(peer)], dst_ref=y_in.at[half, here8],
                send_sem=many.at[5], recv_sem=many.at[6 + half], device_id={"seq": peer}, device_id_type=MESH,
            ).start()
            return 0

        lax.fori_loop(1, SEQ, give, 0)
        pltpu.make_async_copy(y_out.at[half, rows8(seq)], y_in.at[half, here8], many.at[6 + half]).start()

    for half in range(2):
        pltpu.make_async_copy(gate_in.at[half], gate_in.at[half], many.at[3 + half]).wait()
        convolve(2 * half)
        convolve(2 * half + 1)
        give_y(half)

    own_outer.wait()
    arrived(-4, outer.at[:, theirs])
    for half in range(2):
        pltpu.make_async_copy(y_in.at[half], y_in.at[half], many.at[6 + half]).wait()
        for side in range(2):
            cols = slice(side * WIDTH + half * SIDE, side * WIDTH + (half + 1) * SIDE)
            for j in range(2):
                value = outer[j, cols, :] * y_in[half, pl.ds(side * WIDTH + j, SIDE, stride=2), :]
                out[j * SIDE : (j + 1) * SIDE, cols] = value.T

    for copy in started:
        copy.wait_send()
    for number, ref, rows in ((0, filt_t, 8), (2, gate_t, 16), (5, y_out, 8)):
        sent = ref.at[:, pl.ds(rows, 2 * WIDTH - rows)]
        pltpu.make_async_copy(sent, sent, many.at[number]).wait()


SLOTS = 112


def local(tokens, in_weight, short_filter, long_filter, skip_gain):
    width = skip_gain.shape[0]
    weights = in_weight.transpose(1, 0, 2)
    held = tables()
    vmem = pl.BlockSpec(memory_space=pltpu.VMEM)
    anywhere = pl.BlockSpec(memory_space=pl.ANY)
    out = pl.pallas_call(
        kernel,
        out_shape=jax.ShapeDtypeStruct((TOK, width), F32),
        in_specs=[anywhere] * (5 + len(held)),
        out_specs=vmem,
        scratch_shapes=[
            pltpu.VMEM((TOK, width), F32),
            pltpu.VMEM((TAPS, 3, width), F32),
            pltpu.SMEM((width,), F32),
            *[pltpu.VMEM(table.shape, table.dtype) for table in held],
            pltpu.VMEM((BLOCKS, 3, 2 * WROWS, WIDTH), BF16),
            pltpu.VMEM((HALO + POS, CH * FEAT), BF16),
            pltpu.VMEM((HALO + POS, COLS), F32),
            pltpu.VMEM((2, 2 * WIDTH, SIDE), F32),
            pltpu.VMEM((2, 2 * WIDTH, SIDE), F32),
            pltpu.VMEM((2, 2 * WIDTH, SIDE), F32),
            pltpu.VMEM((2, 2 * WIDTH, SIDE), F32),
            pltpu.VMEM((4, WIDTH, SIDE), F32),
            pltpu.VMEM((2, 2 * WIDTH, SIDE), F32),
            pltpu.VMEM((2, 2 * WIDTH, SIDE), F32),
            pltpu.VMEM((2, 2 * WIDTH, SIDE), F32),
            pltpu.VMEM((OWN * SIDE, 2 * SIDE), F32),
            pltpu.SemaphoreType.DMA((SLOTS,)),
            pltpu.SemaphoreType.DMA((SLOTS,)),
            pltpu.SemaphoreType.DMA((8,)),
        ],
        compiler_params=pltpu.CompilerParams(
            collective_id=0, has_side_effects=True, vmem_limit_bytes=60 * 1024 * 1024
        ),
    )(tokens, weights, long_filter, short_filter, skip_gain, *held)
    return out.astype(BF16)


def solution(mesh):
    placed = (P("seq", "ch"), P("seq", None, "ch"), P(None, None, "ch"), P("seq", "ch"), P("ch"))
    return jax.shard_map(
        local, mesh=mesh, in_specs=placed, out_specs=P("seq", "ch"), check_vma=False
    )
```

```python
import math

import jax
import jax.numpy as jnp
import ml_dtypes
import numpy as np
from jax import lax
from jax.experimental import pallas as pl
from jax.experimental.pallas import tpu as pltpu
from jax.sharding import PartitionSpec as P

MESH = pl.DeviceIdType.MESH
BF16, F32 = jnp.bfloat16, jnp.float32

NZ, NY, NX = 8, 4, 4
AROUND = (1, -1, 2, -2)
SEQ, CH = 64, 4
BLOCKS = NZ * NY
TOK = 256
POS = 2 * TOK
FEAT = 1024
HALO = 16
TAPS = 3
WIDTH = 256
COLS = 3 * WIDTH
OWN = 8
WROWS = 64
SPLIT = 48
SIDE = 128
LENGTH = SIDE * SIDE
SPREAD = 27
LO, HI = pl.ds(0, WIDTH // 2), pl.ds(WIDTH // 2, WIDTH // 2)
REST = 2 * WROWS - SPLIT


SWAP, ZF_OWN, ZF_ADDED, ZF, ZFY_OWN, ZFY_ADDED, ZFY, YF, PLANE, TOKEN, CORE, LAST_ROWS, GIVE, RESPOND, PROJECT = (*range(12), 13, 14, 15)


def key(kind, first=0, second=0):
    return 100 * kind + 10 * (first + 4) + second + 4


STEPS = (
    44, 454, 434, 134, 154, 1044, 954, 934, 1304, 1314, 534, 554, 254, 734, 754, 234, 1324, 642, 646, 655,
    653, 364, 633, 635, 324, 1334, 724, 764, 1344, 1354, 1054, 964, 856, 834, 835, 836, 857, 855, 837, 854, 1034,
    924, 1364, 665, 663, 625, 623, 314, 374, 652, 656, 632, 636, 1064, 1024, 1144, 866, 824, 825, 826, 867, 865,
    827, 864, 1444, 662, 626, 622, 666, 615, 613, 304, 675, 673, 384, 1544, 1554, 1534, 876, 814, 815, 877, 875,
    817, 874, 816, 1564, 685, 683, 1524, 612, 672, 616, 676, 886, 804, 805, 887, 885, 884, 806, 807, 682, 686, 1514,
    1574, 1584,
)


def split_table(table):
    high = table.astype(ml_dtypes.bfloat16)
    low = (table - high.astype(np.float64)).astype(ml_dtypes.bfloat16)
    return high, low


def tables():
    slot = np.arange(SIDE)
    n1 = 4 * (slot % BLOCKS) + slot // BLOCKS
    k = np.arange(SIDE)
    outer = 2.0 * math.pi * ((np.outer(4 * k + 1, n1)) % 512) / 512.0
    first = np.concatenate([np.cos(outer), -np.sin(outer)], axis=0)
    last = np.concatenate([np.cos(outer).T, -np.sin(outer).T], axis=1) / LENGTH
    inner = 2.0 * math.pi * (np.outer(k, k) % SIDE) / SIDE
    cos, sin = np.cos(inner), np.sin(inner)
    ahead = np.block([[cos, -sin], [sin, cos]])
    back = np.block([[cos, sin], [-sin, cos]])
    twist = 2.0 * math.pi * np.outer(4 * k + 1, k) / (4.0 * LENGTH)
    fh, fl = split_table(first)
    lh, ll = split_table(last)
    return (
        np.concatenate([fh, fh, fl], axis=1),
        np.concatenate([lh, lh, ll], axis=1),
        np.stack(split_table(ahead)),
        np.stack(split_table(back)),
        np.stack([np.cos(twist), np.sin(twist)]).astype(np.float32),
    )


def halves(values):
    high = values.astype(BF16)
    return high, (values - high.astype(F32)).astype(BF16)


def mm(a, b):
    return jnp.dot(a, b, preferred_element_type=F32)


def right_apply(values, table):
    high, low = halves(values)
    return mm(high, table[0]) + mm(low, table[0]) + mm(high, table[1])


def kernel(
    tokens, weights, filt_hbm, taps_hbm, skip_hbm, first_hbm, last_hbm, ahead_hbm, back_hbm, twist_hbm,
    out,
    filt, taps, skip, first, last, ahead, back, twist,
    w, tok, acc, filt_t, filt_in, gate_t, gate_in, outer_t, outer, y_out, y_in, spec,
    send, recv, many,
):
    seq = lax.axis_index("seq")
    ch = lax.axis_index("ch")
    x_lo, blk = seq % 2, seq // 2
    y, z = blk % NY, blk // NY
    x_hi, core = ch // 2, ch % 2
    x = x_hi * 2 + x_lo

    def seq_of(zz, yy, xx):
        return (zz * NY + yy) * 2 + xx

    def at_yz(dy, dz):
        return {"seq": seq_of((z + dz + NZ) % NZ, (y + dy + NY) % NY, x_lo)}

    def at_x(dx):
        xx = (x + dx + NX) % NX
        return {"seq": seq_of(z, y, xx % 2), "ch": (xx // 2) * 2 + core}

    twin = {"ch": x_hi * 2 + 1 - core}
    mate = {"seq": seq_of(z, y, 1 - x_lo)}

    barrier = pltpu.get_barrier_semaphore()

    def greet(i, _):
        pl.semaphore_signal(barrier, inc=1, device_id={"seq": (seq + i) % SEQ}, device_id_type=MESH)
        return 0

    lax.fori_loop(1, SEQ, greet, 0)
    pl.semaphore_signal(barrier, inc=1, device_id=twin, device_id_type=MESH)
    pl.semaphore_signal(barrier, inc=1, device_id=at_x(3 + 2 * x_lo), device_id_type=MESH)

    started = []
    slots = {}

    def slot(name):
        return slots.setdefault(name, len(slots))

    def go(name, src, dst, device):
        copy = pltpu.make_async_remote_copy(
            src_ref=src, dst_ref=dst, send_sem=send.at[slot(name)], recv_sem=recv.at[slot(name)],
            device_id=device, device_id_type=MESH,
        )
        copy.start()
        started.append(copy)

    def arrived(name, dst):
        pltpu.make_async_copy(dst, dst, recv.at[slot(name)]).wait()

    def local(name, src, dst):
        copy = pltpu.make_async_copy(src, dst, recv.at[slot(name)])
        copy.start()
        return copy

    def block(dy, dz):
        return ((z - dz + NZ) % NZ) * NY + (y - dy + NY) % NY

    early = pl.multiple_of(x_lo * SPLIT, 16)
    late = pl.multiple_of((1 - x_lo) * REST, 16)
    own_rows = pl.ds(pl.multiple_of(x_lo * WROWS, WROWS), WROWS)
    mate_rows = pl.ds(pl.multiple_of((1 - x_lo) * WROWS, WROWS), WROWS)
    added_rows = pl.ds(pl.multiple_of(x_lo * SPLIT + (1 - x_lo) * WROWS, 16), REST - WROWS)

    def yf(dy, lanes=slice(None)):
        return w.at[block(dy, 0), :, pl.ds(late, SPLIT), lanes]

    def yf_plane(dz, piece, lanes=slice(None)):
        return w.at[((z - dz + NZ) % NZ) * NY + piece, :, pl.ds(late, SPLIT), lanes]

    def zf(dy, dz, lanes=slice(None), rows=pl.ds(early, REST)):
        return w.at[block(dy, dz), :, rows, lanes]

    def tk(dx, cc, start=0, rows=TOK):
        xx = (x - dx + NX) % NX
        row = pl.multiple_of(HALO + (xx % 2) * TOK + start, 16)
        col = pl.multiple_of(((xx // 2) * 2 + cc) * FEAT, FEAT)
        return tok.at[pl.ds(row, rows), pl.ds(col, FEAT)]

    HALF = TOK // 2

    mine = pl.ds(pl.multiple_of(x_lo * WIDTH, WIDTH), WIDTH)
    theirs = pl.ds(pl.multiple_of((1 - x_lo) * WIDTH, WIDTH), WIDTH)
    own_w = local(-1, weights.at[:, :, mine], w.at[blk, :, own_rows])
    own_filt = local(-2, filt_hbm, filt)
    own_tok = local(-3, tokens, tk(0, core))
    tables_in = [
        local(name, src, dst)
        for name, src, dst in (
            (-5, first_hbm, first), (-6, last_hbm, last), (-7, ahead_hbm, ahead), (-8, back_hbm, back),
            (-9, twist_hbm, twist), (-10, taps_hbm, taps), (-11, skip_hbm, skip),
        )
    ]

    def rows8(index):
        return pl.ds(pl.multiple_of(index * 8, 8), 8)

    def rows16(index):
        return pl.ds(pl.multiple_of(index * 16, 16), 16)

    own_filt.wait()
    for i in range(4):
        for j in range(2):
            filt_t[i % 2, pl.ds((i // 2) * WIDTH + j, SIDE, stride=2), :] = filt[
                j * 128 : (j + 1) * 128, i * 128 : (i + 1) * 128
            ].T
    pltpu.make_async_copy(filt_t.at[:, rows8(x_lo * BLOCKS + blk)], filt_in.at[:, rows8(seq)], many.at[1]).start()
    own_w.wait()
    pl.semaphore_wait(barrier, SEQ + 1)

    copies = {}

    def plan(name, src, device, after, comes, dst=None):
        copies[name] = (src, src if dst is None else dst, device, after, comes)

    def zf_parts(dz):
        if dz == 0:
            return [key(SWAP)]
        if abs(dz) == 1:
            return [key(ZF_OWN, dz), key(ZF_ADDED, dz)]
        return [key(ZF, 4), key(ZF, -4)] if dz == 4 else [key(ZF, dz)]

    everything = slice(None)
    plan(key(SWAP), weights.at[:, :, theirs], mate, [], w.at[blk, :, mate_rows], w.at[blk, :, own_rows])
    for sign, lanes in ((1, LO), (-1, HI)):
        for own, own_y, rows, after in (
            (ZF_OWN, ZFY_OWN, own_rows, []), (ZF_ADDED, ZFY_ADDED, added_rows, [key(SWAP)]),
        ):
            ref = zf(0, 0, rows=rows)
            plan(key(own, sign), ref, at_yz(0, sign), after, zf(0, sign, rows=rows))
            plan(key(own_y, sign), ref, at_yz(sign, 0), after, zf(sign, 0, rows=rows))
        for dz in (2, 3, 4):
            part = lanes if dz == 4 else everything
            far = sign * dz
            plan(key(ZF, far), zf(0, far - sign, part), at_yz(0, sign), zf_parts(far - sign), zf(0, far, part))
        for dz in range(-3, 5):
            after = [key(ZFY_OWN, sign), key(ZFY_ADDED, sign)]
            if dz != 0:
                after = [key(ZFY, dz, sign)]
                plan(after[0], zf(0, dz), at_yz(sign, 0), zf_parts(dz), zf(sign, dz))
            plan(key(ZFY, dz, 2 * sign), zf(sign, dz, lanes), at_yz(sign, 0), after, zf(2 * sign, dz, lanes))
        plan(key(YF, sign), yf(0), at_yz(sign, 0), [key(SWAP)], yf(sign))
        plan(key(YF, 2 * sign), yf(sign, lanes), at_yz(sign, 0), [key(YF, sign)], yf(2 * sign, lanes))
        for dz in (1, 2, 3, 4):
            part = lanes if dz == 4 else everything
            for piece in range(NY):
                near = sign * (dz - 1)
                after = [key(PLANE, near, piece)] if dz > 1 else [key(YF, by) for by in AROUND]
                plan(
                    key(PLANE, sign * dz, piece), yf_plane(near, piece, part), at_yz(0, sign), after,
                    yf_plane(sign * dz, piece, part),
                )
        start = 0 if sign == 1 else HALF
        plan(key(TOKEN, sign), tokens, at_x(sign), [], tk(sign, core), tk(0, core))
        plan(
            key(TOKEN, 2 * sign), tk(sign, core, start, HALF), at_x(sign), [key(TOKEN, sign)],
            tk(2, core, start, HALF),
        )
        plan(key(CORE, sign), tk(sign, core), twin, [key(TOKEN, sign)], tk(sign, 1 - core))
        plan(
            key(CORE, 2 * sign), tk(2, core, start, HALF), twin, [key(TOKEN, 2 * sign)],
            tk(2, 1 - core, start, HALF),
        )
    plan(key(CORE), tokens, twin, [], tk(0, 1 - core), tk(0, core))
    after = (blk + 1) % BLOCKS
    all_tok = [key(kind, by) for kind in (TOKEN, CORE) for by in AROUND] + [key(CORE)]
    halo = tok.at[pl.ds(0, HALO)]
    plan(key(LAST_ROWS), tok.at[pl.ds(POS, HALO)], {"seq": after * 2 + x_lo}, all_tok, halo, halo)

    here = set()

    def need(names):
        for name in names:
            if name not in here:
                arrived(name, copies[name][4])
                here.add(name)

    def plane_parts(dz):
        parts = zf_parts(dz) + [key(ZFY, dz, by) for by in (2, -2)]
        if dz == 0:
            near = [key(kind, by) for kind in (ZFY_OWN, ZFY_ADDED) for by in (1, -1)]
            return parts + near + [key(YF, by) for by in AROUND]
        ends = (4, -4) if dz == 4 else (dz,)
        parts += [key(ZFY, dz, by) for by in (1, -1)]
        return parts + [key(PLANE, end, piece) for end in ends for piece in range(NY)]

    def project(dz, fresh=False):
        plane = (z - dz + NZ) % NZ

        def part(i, _):
            cols = pl.ds(pl.multiple_of(i * 256, 256), 256)
            term = mm(
                tok[:, pl.ds(pl.multiple_of(plane * 512, 512), 512)],
                w[pl.ds(plane * NY, NY), i].reshape(512, 256),
            )
            acc[:, cols] = term if fresh else acc[:, cols] + term
            return 0

        lax.fori_loop(0, 3, part, 0)

    def give_filter(part):
        def give(i, _):
            peer = (seq + SPREAD * i) % SEQ
            pltpu.make_async_remote_copy(
                src_ref=filt_t.at[:, rows8((peer % 2) * BLOCKS + peer // 2)], dst_ref=filt_in.at[:, rows8(seq)],
                send_sem=many.at[0], recv_sem=many.at[1], device_id={"seq": peer}, device_id_type=MESH,
            ).start()
            return 0

        lax.fori_loop(1 + 9 * part, 10 + 9 * part, give, 0)

    def transform(load, pair):
        columns = jnp.concatenate([load(2 * pair), load(2 * pair + 1)], axis=1)
        high, low = halves(columns)
        turned = mm(first[...], jnp.concatenate([high, low, high], axis=0))
        cos, sin = twist[0], twist[1]
        rows = []
        for i in range(2):
            real = turned[:SIDE, i * SIDE : (i + 1) * SIDE]
            imag = turned[SIDE:, i * SIDE : (i + 1) * SIDE]
            rows.append(jnp.concatenate([real * cos + imag * sin, imag * cos - real * sin], axis=1))
        return right_apply(jnp.concatenate(rows, axis=0), ahead)

    def load_filter(c):
        return jnp.concatenate(
            [
                filt_in[c // 4, pl.ds(8 * (j // 2) + 2 * (c % 4) + j % 2, BLOCKS, stride=16), :]
                for j in range(4)
            ],
            axis=0,
        )

    def load_gate(c):
        return jnp.concatenate(
            [gate_in[c // 4, pl.ds(4 * (c % 4) + j, BLOCKS, stride=16), :] for j in range(4)], axis=0
        )

    def respond():
        for copy in tables_in:
            copy.wait()
        pltpu.make_async_copy(filt_in, filt_in, many.at[1]).wait()
        for pair in range(OWN // 2):
            spec[pair * 256 : (pair + 1) * 256, :] = transform(load_filter, pair)

    fresh = True
    for step in STEPS:
        kind, number = step // 100, step // 10 % 10 - 4
        if step in copies:
            src, dst, device, after, _ = copies[step]
            need(after)
            if kind == LAST_ROWS:
                own_tok.wait()
            go(step, src, dst, device)
        elif kind == PROJECT:
            need([key(LAST_ROWS)] if fresh else [])
            need(plane_parts(number))
            project(number, fresh)
            fresh = False
        elif kind == GIVE:
            give_filter(number + 4)
        else:
            respond()
    assert here == set(copies)

    acc[8:16, :] = jnp.where(blk == 0, 0.0, acc[8:16, :])
    taps_col = pl.ds(pl.multiple_of(x_lo * WIDTH, WIDTH), WIDTH)
    tap = [[taps[j, pl.ds(s, 1), taps_col] for s in range(3)] for j in range(TAPS)]

    def give_gate(half):
        def give(i, _):
            peer = (blk + SPREAD * i) % BLOCKS
            pltpu.make_async_remote_copy(
                src_ref=gate_t.at[half, rows16(peer)], dst_ref=gate_in.at[half, rows16(blk)],
                send_sem=many.at[2], recv_sem=many.at[3 + half], device_id={"seq": peer * 2 + x_lo},
                device_id_type=MESH,
            ).start()
            return 0

        lax.fori_loop(1, BLOCKS, give, 0)
        pltpu.make_async_copy(gate_t.at[half, rows16(blk)], gate_in.at[half, rows16(blk)], many.at[3 + half]).start()

    for stage in range(4):
        half = stage % 2
        lanes = slice(half * SIDE, (half + 1) * SIDE)
        for row in range(4):

            def short(s):
                total = None
                for j in range(TAPS):
                    start = HALO - j + row * SIDE
                    cols = slice(s * WIDTH + half * SIDE, s * WIDTH + (half + 1) * SIDE)
                    term = tap[j][s][:, lanes] * acc[start : start + SIDE, cols]
                    total = term if total is None else total + term
                return total

            if stage < 2:
                gate_t[half, pl.ds(row, SIDE, stride=4), :] = (short(1) * short(2)).T
            else:
                outer_t[row, lanes, :] = short(0).T
        if stage < 2:
            give_gate(half)
    go(-4, outer_t.at[pl.ds(2 * (1 - x_lo), 2)], outer.at[:, mine], mate)
    own_outer = local(-12, outer_t.at[pl.ds(2 * x_lo, 2)], outer.at[:, mine])

    def all_sent(number, ref, rows):
        sent = ref.at[:, pl.ds(rows, 2 * WIDTH - rows)]
        pltpu.make_async_copy(sent, sent, many.at[number]).wait()

    for copy in started[:-1]:
        copy.wait_send()
    all_sent(0, filt_t, 8)

    def convolve(pair):
        spectrum = transform(load_gate, pair)
        response = spec[pair * 256 : (pair + 1) * 256, :]
        sr, si = spectrum[:, :SIDE], spectrum[:, SIDE:]
        rr, ri = response[:, :SIDE], response[:, SIDE:]
        product = jnp.concatenate([sr * rr - si * ri, sr * ri + si * rr], axis=1)
        inverse = right_apply(product, back)
        cos, sin = twist[0], twist[1]
        cols = []
        for i in range(2):
            real = inverse[i * SIDE : (i + 1) * SIDE, :SIDE]
            imag = inverse[i * SIDE : (i + 1) * SIDE, SIDE:]
            cols.append(jnp.concatenate([real * cos - imag * sin, imag * cos + real * sin], axis=0))
        high, low = halves(jnp.concatenate(cols, axis=1))
        result = mm(last[...], jnp.concatenate([high, low, high], axis=0))
        for i in range(2):
            c = 2 * pair + i
            gain = skip[x_lo * WIDTH + (c // 4) * SIDE + blk * 4 + c % 4]
            total = result[:, i * SIDE : (i + 1) * SIDE] + gain * load_gate(c)
            for j in range(4):
                place = pl.ds(8 * (j // 2) + 2 * (c % 4) + j % 2, BLOCKS, stride=16)
                y_out[c // 4, place, :] = total[j * BLOCKS : (j + 1) * BLOCKS, :]

    def give_y(half):
        here8 = rows8(x_lo * BLOCKS + blk)

        def give(i, _):
            peer = (seq + SPREAD * i) % SEQ
            pltpu.make_async_remote_copy(
                src_ref=y_out.at[half, rows8(peer)], dst_ref=y_in.at[half, here8],
                send_sem=many.at[5], recv_sem=many.at[6 + half], device_id={"seq": peer}, device_id_type=MESH,
            ).start()
            return 0

        lax.fori_loop(1, SEQ, give, 0)
        pltpu.make_async_copy(y_out.at[half, rows8(seq)], y_in.at[half, here8], many.at[6 + half]).start()

    for half in range(2):
        pltpu.make_async_copy(gate_in.at[half], gate_in.at[half], many.at[3 + half]).wait()
        convolve(2 * half)
        convolve(2 * half + 1)
        give_y(half)

    started[-1].wait_send()
    all_sent(2, gate_t, 16)
    own_outer.wait()
    arrived(-4, outer.at[:, theirs])
    for half in range(2):
        pltpu.make_async_copy(y_in.at[half], y_in.at[half], many.at[6 + half]).wait()
        for side in range(2):
            cols = slice(side * WIDTH + half * SIDE, side * WIDTH + (half + 1) * SIDE)
            for j in range(2):
                value = outer[j, cols, :] * y_in[half, pl.ds(side * WIDTH + j, SIDE, stride=2), :]
                out[j * SIDE : (j + 1) * SIDE, cols] = value.T

    all_sent(5, y_out, 8)


SLOTS = 112


def local(tokens, in_weight, short_filter, long_filter, skip_gain):
    width = skip_gain.shape[0]
    weights = in_weight.transpose(1, 0, 2)
    held = tables()
    vmem = pl.BlockSpec(memory_space=pltpu.VMEM)
    anywhere = pl.BlockSpec(memory_space=pl.ANY)
    out = pl.pallas_call(
        kernel,
        out_shape=jax.ShapeDtypeStruct((TOK, width), F32),
        in_specs=[anywhere] * (5 + len(held)),
        out_specs=vmem,
        scratch_shapes=[
            pltpu.VMEM((TOK, width), F32),
            pltpu.VMEM((TAPS, 3, width), F32),
            pltpu.SMEM((width,), F32),
            *[pltpu.VMEM(table.shape, table.dtype) for table in held],
            pltpu.VMEM((BLOCKS, 3, 2 * WROWS, WIDTH), BF16),
            pltpu.VMEM((HALO + POS, CH * FEAT), BF16),
            pltpu.VMEM((HALO + POS, COLS), F32),
            pltpu.VMEM((2, 2 * WIDTH, SIDE), F32),
            pltpu.VMEM((2, 2 * WIDTH, SIDE), F32),
            pltpu.VMEM((2, 2 * WIDTH, SIDE), F32),
            pltpu.VMEM((2, 2 * WIDTH, SIDE), F32),
            pltpu.VMEM((4, WIDTH, SIDE), F32),
            pltpu.VMEM((2, 2 * WIDTH, SIDE), F32),
            pltpu.VMEM((2, 2 * WIDTH, SIDE), F32),
            pltpu.VMEM((2, 2 * WIDTH, SIDE), F32),
            pltpu.VMEM((OWN * SIDE, 2 * SIDE), F32),
            pltpu.SemaphoreType.DMA((SLOTS,)),
            pltpu.SemaphoreType.DMA((SLOTS,)),
            pltpu.SemaphoreType.DMA((8,)),
        ],
        compiler_params=pltpu.CompilerParams(
            collective_id=0, has_side_effects=True, vmem_limit_bytes=60 * 1024 * 1024
        ),
    )(tokens, weights, long_filter, short_filter, skip_gain, *held)
    return out.astype(BF16)


def solution(mesh):
    placed = (P("seq", "ch"), P("seq", None, "ch"), P(None, None, "ch"), P("seq", "ch"), P("ch"))
    return jax.shard_map(
        local, mesh=mesh, in_specs=placed, out_specs=P("seq", "ch"), check_vma=False
    )
```

```python
import math

import jax
import jax.numpy as jnp
import ml_dtypes
import numpy as np
from jax import lax
from jax.experimental import pallas as pl
from jax.experimental.pallas import tpu as pltpu
from jax.sharding import PartitionSpec as P

MESH = pl.DeviceIdType.MESH
BF16, F32 = jnp.bfloat16, jnp.float32

NZ, NY, NX = 8, 4, 4
AROUND = (1, -1, 2, -2)
SEQ, CH = 64, 4
BLOCKS = NZ * NY
TOK = 256
POS = 2 * TOK
FEAT = 1024
HALO = 16
TAPS = 3
WIDTH = 256
COLS = 3 * WIDTH
OWN = 8
WROWS = 64
SPLIT = 48
SIDE = 128
LENGTH = SIDE * SIDE
SPREAD = 27
ROWS = 512
LO, HI = pl.ds(0, WIDTH // 2), pl.ds(WIDTH // 2, WIDTH // 2)
REST = 2 * WROWS - SPLIT


SWAP, ZF_OWN, ZF_ADDED, ZF, ZFY_OWN, ZFY_ADDED, ZFY, YF, PLANE, TOKEN, CORE, LAST_ROWS, GIVE, RESPOND, PROJECT = (*range(12), 13, 14, 15)


def key(kind, first=0, second=0):
    return 100 * kind + 10 * (first + 4) + second + 4


STEPS = (
    44, 454, 434, 134, 154, 1044, 954, 934, 1304, 1314, 534, 554, 254, 734, 754, 234, 1324, 642, 646, 655,
    653, 364, 633, 635, 324, 1334, 724, 764, 1344, 1354, 1054, 964, 856, 834, 835, 836, 857, 855, 837, 854, 1034,
    924, 1364, 665, 663, 625, 623, 314, 374, 652, 656, 632, 636, 1064, 1024, 1144, 866, 824, 825, 826, 867, 865,
    827, 864, 1444, 662, 626, 622, 666, 615, 613, 304, 675, 673, 384, 1544, 1554, 1534, 876, 814, 815, 877, 875,
    817, 874, 816, 1564, 685, 683, 1524, 612, 672, 616, 676, 886, 804, 805, 887, 885, 884, 806, 807, 682, 686, 1514,
    1574, 1584,
)


def split_table(table):
    high = table.astype(ml_dtypes.bfloat16)
    low = (table - high.astype(np.float64)).astype(ml_dtypes.bfloat16)
    return high, low


def tables():
    slot = np.arange(SIDE)
    n1 = 4 * (slot % BLOCKS) + slot // BLOCKS
    k = np.arange(SIDE)
    outer = 2.0 * math.pi * ((np.outer(4 * k + 1, n1)) % 512) / 512.0
    first = np.concatenate([np.cos(outer), -np.sin(outer)], axis=0)
    last = np.concatenate([np.cos(outer).T, -np.sin(outer).T], axis=1) / LENGTH
    inner = 2.0 * math.pi * (np.outer(k, k) % SIDE) / SIDE
    cos, sin = np.cos(inner), np.sin(inner)
    ahead = np.block([[cos, -sin], [sin, cos]])
    back = np.block([[cos, sin], [-sin, cos]])
    twist = 2.0 * math.pi * np.outer(4 * k + 1, k) / (4.0 * LENGTH)
    fh, fl = split_table(first)
    lh, ll = split_table(last)
    return (
        np.concatenate([fh, fh, fl], axis=1),
        np.concatenate([lh, lh, ll], axis=1),
        np.stack(split_table(ahead)),
        np.stack(split_table(back)),
        np.stack([np.cos(twist), np.sin(twist)]).astype(np.float32),
    )


def halves(values):
    high = values.astype(BF16)
    return high, (values - high.astype(F32)).astype(BF16)


def mm(a, b):
    return jnp.dot(a, b, preferred_element_type=F32)


def right_apply(values, table):
    high, low = halves(values)
    return mm(high, table[0]) + mm(low, table[0]) + mm(high, table[1])


def kernel(
    tokens, weights, filt_hbm, taps_hbm, skip_hbm, first_hbm, last_hbm, ahead_hbm, back_hbm, twist_hbm,
    out,
    filt, taps, skip, first, last, ahead, back, twist,
    w, tok, acc, filt_t, filt_in, gate_t, gate_in, outer_t, outer, y_out, y_in, spec,
    send, recv, many,
):
    seq = lax.axis_index("seq")
    ch = lax.axis_index("ch")
    x_lo, blk = seq % 2, seq // 2
    y, z = blk % NY, blk // NY
    x_hi, core = ch // 2, ch % 2
    x = x_hi * 2 + x_lo

    def seq_of(zz, yy, xx):
        return (zz * NY + yy) * 2 + xx

    def at_yz(dy, dz):
        return {"seq": seq_of((z + dz + NZ) % NZ, (y + dy + NY) % NY, x_lo)}

    def at_x(dx):
        xx = (x + dx + NX) % NX
        return {"seq": seq_of(z, y, xx % 2), "ch": (xx // 2) * 2 + core}

    twin = {"ch": x_hi * 2 + 1 - core}
    mate = {"seq": seq_of(z, y, 1 - x_lo)}

    barrier = pltpu.get_barrier_semaphore()

    def greet(i, _):
        pl.semaphore_signal(barrier, inc=1, device_id={"seq": (seq + i) % SEQ}, device_id_type=MESH)
        return 0

    lax.fori_loop(1, SEQ, greet, 0)
    pl.semaphore_signal(barrier, inc=1, device_id=twin, device_id_type=MESH)
    pl.semaphore_signal(barrier, inc=1, device_id=at_x(3 + 2 * x_lo), device_id_type=MESH)

    started = []
    slots = {}

    def slot(name):
        return slots.setdefault(name, len(slots))

    def go(name, src, dst, device):
        copy = pltpu.make_async_remote_copy(
            src_ref=src, dst_ref=dst, send_sem=send.at[slot(name)], recv_sem=recv.at[slot(name)],
            device_id=device, device_id_type=MESH,
        )
        copy.start()
        started.append(copy)

    def arrived(name, dst):
        pltpu.make_async_copy(dst, dst, recv.at[slot(name)]).wait()

    def local(name, src, dst):
        copy = pltpu.make_async_copy(src, dst, recv.at[slot(name)])
        copy.start()
        return copy

    def block(dy, dz):
        return ((z - dz + NZ) % NZ) * NY + (y - dy + NY) % NY

    early = pl.multiple_of(x_lo * SPLIT, 16)
    late = pl.multiple_of((1 - x_lo) * REST, 16)
    own_rows = pl.ds(pl.multiple_of(x_lo * WROWS, WROWS), WROWS)
    mate_rows = pl.ds(pl.multiple_of((1 - x_lo) * WROWS, WROWS), WROWS)
    added_rows = pl.ds(pl.multiple_of(x_lo * SPLIT + (1 - x_lo) * WROWS, 16), REST - WROWS)

    def yf(dy, lanes=slice(None)):
        return w.at[block(dy, 0), :, pl.ds(late, SPLIT), lanes]

    def yf_plane(dz, piece, lanes=slice(None)):
        return w.at[((z - dz + NZ) % NZ) * NY + piece, :, pl.ds(late, SPLIT), lanes]

    def zf(dy, dz, lanes=slice(None), rows=pl.ds(early, REST)):
        return w.at[block(dy, dz), :, rows, lanes]

    def tk(dx, cc, start=0, rows=TOK):
        xx = (x - dx + NX) % NX
        row = pl.multiple_of(HALO + (xx % 2) * TOK + start, 16)
        col = pl.multiple_of(((xx // 2) * 2 + cc) * FEAT, FEAT)
        return tok.at[pl.ds(row, rows), pl.ds(col, FEAT)]

    HALF = TOK // 2

    mine = pl.ds(pl.multiple_of(x_lo * WIDTH, WIDTH), WIDTH)
    theirs = pl.ds(pl.multiple_of((1 - x_lo) * WIDTH, WIDTH), WIDTH)
    own_w = local(-1, weights.at[:, :, mine], w.at[blk, :, own_rows])
    own_filt = local(-2, filt_hbm, filt)
    own_tok = local(-3, tokens, tk(0, core))
    tables_in = [
        local(name, src, dst)
        for name, src, dst in (
            (-5, first_hbm, first), (-6, last_hbm, last), (-7, ahead_hbm, ahead), (-8, back_hbm, back),
            (-9, twist_hbm, twist), (-10, taps_hbm, taps), (-11, skip_hbm, skip),
        )
    ]

    def rows8(index):
        return pl.ds(pl.multiple_of(index * 8, 8), 8)

    def rows16(index):
        return pl.ds(pl.multiple_of(index * 16, 16), 16)

    own_filt.wait()
    for i in range(4):
        for j in range(2):
            filt_t[i % 2, pl.ds((i // 2) * WIDTH + j, SIDE, stride=2), :] = filt[
                j * 128 : (j + 1) * 128, i * 128 : (i + 1) * 128
            ].T
    pltpu.make_async_copy(filt_t.at[:, rows8(x_lo * BLOCKS + blk)], filt_in.at[:, rows8(seq)], many.at[1]).start()
    own_w.wait()
    pl.semaphore_wait(barrier, SEQ + 1)

    copies = {}

    def plan(name, src, device, after, comes, dst=None):
        copies[name] = (src, src if dst is None else dst, device, after, comes)

    def zf_parts(dz):
        if dz == 0:
            return [key(SWAP)]
        if abs(dz) == 1:
            return [key(ZF_OWN, dz), key(ZF_ADDED, dz)]
        return [key(ZF, 4), key(ZF, -4)] if dz == 4 else [key(ZF, dz)]

    everything = slice(None)
    plan(key(SWAP), weights.at[:, :, theirs], mate, [], w.at[blk, :, mate_rows], w.at[blk, :, own_rows])
    for sign, lanes in ((1, LO), (-1, HI)):
        for own, own_y, rows, after in (
            (ZF_OWN, ZFY_OWN, own_rows, []), (ZF_ADDED, ZFY_ADDED, added_rows, [key(SWAP)]),
        ):
            ref = zf(0, 0, rows=rows)
            plan(key(own, sign), ref, at_yz(0, sign), after, zf(0, sign, rows=rows))
            plan(key(own_y, sign), ref, at_yz(sign, 0), after, zf(sign, 0, rows=rows))
        for dz in (2, 3, 4):
            part = lanes if dz == 4 else everything
            far = sign * dz
            plan(key(ZF, far), zf(0, far - sign, part), at_yz(0, sign), zf_parts(far - sign), zf(0, far, part))
        for dz in range(-3, 5):
            after = [key(ZFY_OWN, sign), key(ZFY_ADDED, sign)]
            if dz != 0:
                after = [key(ZFY, dz, sign)]
                plan(after[0], zf(0, dz), at_yz(sign, 0), zf_parts(dz), zf(sign, dz))
            plan(key(ZFY, dz, 2 * sign), zf(sign, dz, lanes), at_yz(sign, 0), after, zf(2 * sign, dz, lanes))
        plan(key(YF, sign), yf(0), at_yz(sign, 0), [key(SWAP)], yf(sign))
        plan(key(YF, 2 * sign), yf(sign, lanes), at_yz(sign, 0), [key(YF, sign)], yf(2 * sign, lanes))
        for dz in (1, 2, 3, 4):
            part = lanes if dz == 4 else everything
            for piece in range(NY):
                near = sign * (dz - 1)
                after = [key(PLANE, near, piece)] if dz > 1 else [key(YF, by) for by in AROUND]
                plan(
                    key(PLANE, sign * dz, piece), yf_plane(near, piece, part), at_yz(0, sign), after,
                    yf_plane(sign * dz, piece, part),
                )
        start = 0 if sign == 1 else HALF
        plan(key(TOKEN, sign), tokens, at_x(sign), [], tk(sign, core), tk(0, core))
        plan(
            key(TOKEN, 2 * sign), tk(sign, core, start, HALF), at_x(sign), [key(TOKEN, sign)],
            tk(2, core, start, HALF),
        )
        plan(key(CORE, sign), tk(sign, core), twin, [key(TOKEN, sign)], tk(sign, 1 - core))
        plan(
            key(CORE, 2 * sign), tk(2, core, start, HALF), twin, [key(TOKEN, 2 * sign)],
            tk(2, 1 - core, start, HALF),
        )
    plan(key(CORE), tokens, twin, [], tk(0, 1 - core), tk(0, core))
    after = (blk + 1) % BLOCKS
    all_tok = [key(kind, by) for kind in (TOKEN, CORE) for by in AROUND] + [key(CORE)]
    halo = tok.at[pl.ds(0, HALO)]
    plan(key(LAST_ROWS), tok.at[pl.ds(POS, HALO)], {"seq": after * 2 + x_lo}, all_tok, halo, halo)

    here = set()

    def need(names):
        for name in names:
            if name not in here:
                arrived(name, copies[name][4])
                here.add(name)

    def plane_parts(dz):
        parts = zf_parts(dz) + [key(ZFY, dz, by) for by in (2, -2)]
        if dz == 0:
            near = [key(kind, by) for kind in (ZFY_OWN, ZFY_ADDED) for by in (1, -1)]
            return parts + near + [key(YF, by) for by in AROUND]
        ends = (4, -4) if dz == 4 else (dz,)
        parts += [key(ZFY, dz, by) for by in (1, -1)]
        return parts + [key(PLANE, end, piece) for end in ends for piece in range(NY)]

    def project(dz, fresh=False):
        plane = (z - dz + NZ) % NZ

        def part(i, _):
            cols = pl.ds(pl.multiple_of(i * 256, 256), 256)
            term = mm(
                tok[:, pl.ds(pl.multiple_of(plane * 512, 512), 512)],
                w[pl.ds(plane * NY, NY), i].reshape(512, 256),
            )
            acc[:, cols] = term if fresh else acc[:, cols] + term
            return 0

        lax.fori_loop(0, 3, part, 0)

    def give_filter(part):
        def give(i, _):
            peer = (seq + SPREAD * i) % SEQ
            pltpu.make_async_remote_copy(
                src_ref=filt_t.at[:, rows8((peer % 2) * BLOCKS + peer // 2)], dst_ref=filt_in.at[:, rows8(seq)],
                send_sem=many.at[0], recv_sem=many.at[1], device_id={"seq": peer}, device_id_type=MESH,
            ).start()
            return 0

        lax.fori_loop(1 + 9 * part, 10 + 9 * part, give, 0)

    def transform(load, pair):
        columns = jnp.concatenate([load(2 * pair), load(2 * pair + 1)], axis=1)
        high, low = halves(columns)
        turned = mm(first[...], jnp.concatenate([high, low, high], axis=0))
        cos, sin = twist[0], twist[1]
        rows = []
        for i in range(2):
            real = turned[:SIDE, i * SIDE : (i + 1) * SIDE]
            imag = turned[SIDE:, i * SIDE : (i + 1) * SIDE]
            rows.append(jnp.concatenate([real * cos + imag * sin, imag * cos - real * sin], axis=1))
        return right_apply(jnp.concatenate(rows, axis=0), ahead)

    def load_filter(c):
        return jnp.concatenate(
            [
                filt_in[c // 4, pl.ds(8 * (j // 2) + 2 * (c % 4) + j % 2, BLOCKS, stride=16), :]
                for j in range(4)
            ],
            axis=0,
        )

    def load_gate(c):
        return jnp.concatenate(
            [gate_in[c // 4, pl.ds(4 * (c % 4) + j, BLOCKS, stride=16), :] for j in range(4)], axis=0
        )

    def respond():
        for copy in tables_in:
            copy.wait()
        whole = filt_in.at[:, pl.ds(0, ROWS)]
        pltpu.make_async_copy(whole, whole, many.at[1]).wait()
        for pair in range(OWN // 2):
            spec[pair * 256 : (pair + 1) * 256, :] = transform(load_filter, pair)

    fresh = True
    for step in STEPS:
        kind, number = step // 100, step // 10 % 10 - 4
        if step in copies:
            src, dst, device, after, _ = copies[step]
            need(after)
            if kind == LAST_ROWS:
                own_tok.wait()
            go(step, src, dst, device)
        elif kind == PROJECT:
            need([key(LAST_ROWS)] if fresh else [])
            need(plane_parts(number))
            project(number, fresh)
            fresh = False
        elif kind == GIVE:
            give_filter(number + 4)
        else:
            respond()
    assert here == set(copies)

    acc[8:16, :] = jnp.where(blk == 0, 0.0, acc[8:16, :])
    taps_col = pl.ds(pl.multiple_of(x_lo * WIDTH, WIDTH), WIDTH)
    tap = [[taps[j, pl.ds(s, 1), taps_col] for s in range(3)] for j in range(TAPS)]

    def give_gate(half):
        def give(i, _):
            peer = (blk + SPREAD * i) % BLOCKS
            pltpu.make_async_remote_copy(
                src_ref=gate_t.at[half, rows16(peer)], dst_ref=gate_in.at[half, rows16(blk)],
                send_sem=many.at[2], recv_sem=many.at[3 + half], device_id={"seq": peer * 2 + x_lo},
                device_id_type=MESH,
            ).start()
            return 0

        lax.fori_loop(1, BLOCKS, give, 0)
        pltpu.make_async_copy(gate_t.at[half, rows16(blk)], gate_in.at[half, rows16(blk)], many.at[3 + half]).start()

    for stage in range(4):
        half = stage % 2
        lanes = slice(half * SIDE, (half + 1) * SIDE)
        for row in range(4):

            def short(s):
                total = None
                for j in range(TAPS):
                    start = HALO - j + row * SIDE
                    cols = slice(s * WIDTH + half * SIDE, s * WIDTH + (half + 1) * SIDE)
                    term = tap[j][s][:, lanes] * acc[start : start + SIDE, cols]
                    total = term if total is None else total + term
                return total

            if stage < 2:
                gate_t[half, pl.ds(row, SIDE, stride=4), :] = (short(1) * short(2)).T
            else:
                outer_t[row, lanes, :] = short(0).T
        if stage < 2:
            give_gate(half)
    go(-4, outer_t.at[pl.ds(2 * (1 - x_lo), 2)], outer.at[:, mine], mate)
    own_outer = local(-12, outer_t.at[pl.ds(2 * x_lo, 2)], outer.at[:, mine])

    def all_sent(number, ref, rows):
        sent = ref.at[:, pl.ds(rows, ROWS - rows)]
        pltpu.make_async_copy(sent, sent, many.at[number]).wait()

    for copy in started[:-1]:
        copy.wait_send()
    all_sent(0, filt_t, 8)

    def convolve(pair):
        spectrum = transform(load_gate, pair)
        response = spec[pair * 256 : (pair + 1) * 256, :]
        sr, si = spectrum[:, :SIDE], spectrum[:, SIDE:]
        rr, ri = response[:, :SIDE], response[:, SIDE:]
        product = jnp.concatenate([sr * rr - si * ri, sr * ri + si * rr], axis=1)
        inverse = right_apply(product, back)
        cos, sin = twist[0], twist[1]
        cols = []
        for i in range(2):
            real = inverse[i * SIDE : (i + 1) * SIDE, :SIDE]
            imag = inverse[i * SIDE : (i + 1) * SIDE, SIDE:]
            cols.append(jnp.concatenate([real * cos - imag * sin, imag * cos + real * sin], axis=0))
        high, low = halves(jnp.concatenate(cols, axis=1))
        result = mm(last[...], jnp.concatenate([high, low, high], axis=0))
        for i in range(2):
            c = 2 * pair + i
            gain = skip[x_lo * WIDTH + (c // 4) * SIDE + blk * 4 + c % 4]
            total = result[:, i * SIDE : (i + 1) * SIDE] + gain * load_gate(c)
            for j in range(4):
                place = pl.ds(8 * (j // 2) + 2 * (c % 4) + j % 2, BLOCKS, stride=16)
                y_out[c // 4, place, :] = total[j * BLOCKS : (j + 1) * BLOCKS, :]

    def give_y(half):
        here8 = rows8(x_lo * BLOCKS + blk)

        def give(i, _):
            peer = (seq + SPREAD * i) % SEQ
            pltpu.make_async_remote_copy(
                src_ref=y_out.at[half, rows8(peer)], dst_ref=y_in.at[half, here8],
                send_sem=many.at[5], recv_sem=many.at[6 + half], device_id={"seq": peer}, device_id_type=MESH,
            ).start()
            return 0

        lax.fori_loop(1, SEQ, give, 0)
        pltpu.make_async_copy(y_out.at[half, rows8(seq)], y_in.at[half, here8], many.at[6 + half]).start()

    for half in range(2):
        whole = gate_in.at[half, pl.ds(0, ROWS)]
        pltpu.make_async_copy(whole, whole, many.at[3 + half]).wait()
        convolve(2 * half)
        convolve(2 * half + 1)
        give_y(half)

    started[-1].wait_send()
    all_sent(2, gate_t, 16)
    own_outer.wait()
    arrived(-4, outer.at[:, theirs])
    for half in range(2):
        whole = y_in.at[half, pl.ds(0, ROWS)]
        pltpu.make_async_copy(whole, whole, many.at[6 + half]).wait()
        for side in range(2):
            cols = slice(side * WIDTH + half * SIDE, side * WIDTH + (half + 1) * SIDE)
            for j in range(2):
                value = outer[j, cols, :] * y_in[half, pl.ds(side * WIDTH + j, SIDE, stride=2), :]
                out[j * SIDE : (j + 1) * SIDE, cols] = value.T

    all_sent(5, y_out, 8)


SLOTS = 112


def local(tokens, in_weight, short_filter, long_filter, skip_gain):
    width = skip_gain.shape[0]
    weights = in_weight.transpose(1, 0, 2)
    held = tables()
    vmem = pl.BlockSpec(memory_space=pltpu.VMEM)
    anywhere = pl.BlockSpec(memory_space=pl.ANY)
    out = pl.pallas_call(
        kernel,
        out_shape=jax.ShapeDtypeStruct((TOK, width), F32),
        in_specs=[anywhere] * (5 + len(held)),
        out_specs=vmem,
        scratch_shapes=[
            pltpu.VMEM((TOK, width), F32),
            pltpu.VMEM((TAPS, 3, width), F32),
            pltpu.SMEM((width,), F32),
            *[pltpu.VMEM(table.shape, table.dtype) for table in held],
            pltpu.VMEM((BLOCKS, 3, 2 * WROWS, WIDTH), BF16),
            pltpu.VMEM((HALO + POS, CH * FEAT), BF16),
            pltpu.VMEM((HALO + POS, COLS), F32),
            pltpu.VMEM((2, ROWS + 16, SIDE), F32),
            pltpu.VMEM((2, ROWS + 16, SIDE), F32),
            pltpu.VMEM((2, ROWS + 16, SIDE), F32),
            pltpu.VMEM((2, ROWS + 16, SIDE), F32),
            pltpu.VMEM((4, WIDTH, SIDE), F32),
            pltpu.VMEM((2, 2 * WIDTH, SIDE), F32),
            pltpu.VMEM((2, ROWS + 16, SIDE), F32),
            pltpu.VMEM((2, ROWS + 16, SIDE), F32),
            pltpu.VMEM((OWN * SIDE, 2 * SIDE), F32),
            pltpu.SemaphoreType.DMA((SLOTS,)),
            pltpu.SemaphoreType.DMA((SLOTS,)),
            pltpu.SemaphoreType.DMA((8,)),
        ],
        compiler_params=pltpu.CompilerParams(
            collective_id=0, has_side_effects=True, vmem_limit_bytes=60 * 1024 * 1024
        ),
    )(tokens, weights, long_filter, short_filter, skip_gain, *held)
    return out.astype(BF16)


def solution(mesh):
    placed = (P("seq", "ch"), P("seq", None, "ch"), P(None, None, "ch"), P("seq", "ch"), P("ch"))
    return jax.shard_map(
        local, mesh=mesh, in_specs=placed, out_specs=P("seq", "ch"), check_vma=False
    )
```

```python
import math

import jax
import jax.numpy as jnp
import ml_dtypes
import numpy as np
from jax import lax
from jax.experimental import pallas as pl
from jax.experimental.pallas import tpu as pltpu
from jax.sharding import PartitionSpec as P

MESH = pl.DeviceIdType.MESH
BF16, F32 = jnp.bfloat16, jnp.float32

NZ, NY, NX = 8, 4, 4
AROUND = (1, -1, 2, -2)
SEQ, CH = 64, 4
BLOCKS = NZ * NY
TOK = 256
POS = 2 * TOK
FEAT = 1024
HALO = 16
TAPS = 3
WIDTH = 256
COLS = 3 * WIDTH
OWN = 8
WROWS = 64
SPLIT = 48
SIDE = 128
LENGTH = SIDE * SIDE
SPREAD = 27
ROWS = 512
LO, HI = pl.ds(0, WIDTH // 2), pl.ds(WIDTH // 2, WIDTH // 2)
REST = 2 * WROWS - SPLIT


SWAP, ZF_OWN, ZF_ADDED, ZF, ZFY_OWN, ZFY_ADDED, ZFY, YF, PLANE, TOKEN, CORE, LAST_ROWS, GIVE, RESPOND, PROJECT = (*range(12), 13, 14, 15)


def key(kind, first=0, second=0):
    return 100 * kind + 10 * (first + 4) + second + 4


STEPS = (
    44, 454, 434, 134, 154, 1044, 954, 934, 1304, 1314, 534, 554, 254, 734, 754, 234, 1324, 642, 646, 655,
    653, 364, 633, 635, 324, 1334, 724, 764, 1344, 1354, 1054, 964, 856, 834, 835, 836, 857, 855, 837, 854, 1034,
    924, 1364, 665, 663, 625, 623, 314, 374, 652, 656, 632, 636, 1064, 1024, 1144, 866, 824, 825, 826, 867, 865,
    827, 864, 1444, 662, 626, 622, 666, 615, 613, 304, 675, 673, 384, 1544, 1554, 1534, 876, 814, 815, 877, 875,
    817, 874, 816, 1564, 685, 683, 1524, 612, 672, 616, 676, 886, 804, 805, 887, 885, 884, 806, 807, 682, 686, 1514,
    1574, 1584,
)


def split_table(table):
    high = table.astype(ml_dtypes.bfloat16)
    low = (table - high.astype(np.float64)).astype(ml_dtypes.bfloat16)
    return high, low


def tables():
    slot = np.arange(SIDE)
    n1 = 4 * (slot % BLOCKS) + slot // BLOCKS
    k = np.arange(SIDE)
    outer = 2.0 * math.pi * ((np.outer(4 * k + 1, n1)) % 512) / 512.0
    first = np.concatenate([np.cos(outer), -np.sin(outer)], axis=0)
    last = np.concatenate([np.cos(outer).T, -np.sin(outer).T], axis=1) / LENGTH
    inner = 2.0 * math.pi * (np.outer(k, k) % SIDE) / SIDE
    cos, sin = np.cos(inner), np.sin(inner)
    ahead = np.block([[cos, -sin], [sin, cos]])
    back = np.block([[cos, sin], [-sin, cos]])
    twist = 2.0 * math.pi * np.outer(4 * k + 1, k) / (4.0 * LENGTH)
    fh, fl = split_table(first)
    lh, ll = split_table(last)
    return (
        np.concatenate([fh, fh, fl], axis=1),
        np.concatenate([lh, lh, ll], axis=1),
        np.stack(split_table(ahead)),
        np.stack(split_table(back)),
        np.stack([np.cos(twist), np.sin(twist)]).astype(np.float32),
    )


def halves(values):
    high = values.astype(BF16)
    return high, (values - high.astype(F32)).astype(BF16)


def mm(a, b):
    return jnp.dot(a, b, preferred_element_type=F32)


def right_apply(values, table):
    high, low = halves(values)
    return mm(high, table[0]) + mm(low, table[0]) + mm(high, table[1])


def kernel(
    tokens, weights, filt_hbm, taps_hbm, skip_hbm, first_hbm, last_hbm, ahead_hbm, back_hbm, twist_hbm,
    out,
    filt, taps, skip, first, last, ahead, back, twist,
    w, tok, acc, filt_t, filt_in, gate_t, gate_in, outer_t, outer, y_out, y_in, spec,
    send, recv, many,
):
    seq = lax.axis_index("seq")
    ch = lax.axis_index("ch")
    x_lo, blk = seq % 2, seq // 2
    y, z = blk % NY, blk // NY
    x_hi, core = ch // 2, ch % 2
    x = x_hi * 2 + x_lo

    def seq_of(zz, yy, xx):
        return (zz * NY + yy) * 2 + xx

    def at_yz(dy, dz):
        return {"seq": seq_of((z + dz + NZ) % NZ, (y + dy + NY) % NY, x_lo)}

    def at_x(dx):
        xx = (x + dx + NX) % NX
        return {"seq": seq_of(z, y, xx % 2), "ch": (xx // 2) * 2 + core}

    twin = {"ch": x_hi * 2 + 1 - core}
    mate = {"seq": seq_of(z, y, 1 - x_lo)}

    barrier = pltpu.get_barrier_semaphore()

    def greet(i, _):
        pl.semaphore_signal(barrier, inc=1, device_id={"seq": (seq + i) % SEQ}, device_id_type=MESH)
        return 0

    lax.fori_loop(1, SEQ, greet, 0)
    pl.semaphore_signal(barrier, inc=1, device_id=twin, device_id_type=MESH)
    pl.semaphore_signal(barrier, inc=1, device_id=at_x(3 + 2 * x_lo), device_id_type=MESH)

    started = []
    slots = {}

    def slot(name):
        return slots.setdefault(name, len(slots))

    def go(name, src, dst, device):
        copy = pltpu.make_async_remote_copy(
            src_ref=src, dst_ref=dst, send_sem=send.at[slot(name)], recv_sem=recv.at[slot(name)],
            device_id=device, device_id_type=MESH,
        )
        copy.start()
        started.append(copy)

    def arrived(name, dst):
        pltpu.make_async_copy(dst, dst, recv.at[slot(name)]).wait()

    def local(name, src, dst):
        copy = pltpu.make_async_copy(src, dst, recv.at[slot(name)])
        copy.start()
        return copy

    def block(dy, dz):
        return ((z - dz + NZ) % NZ) * NY + (y - dy + NY) % NY

    early = pl.multiple_of(x_lo * SPLIT, 16)
    late = pl.multiple_of((1 - x_lo) * REST, 16)
    own_rows = pl.ds(pl.multiple_of(x_lo * WROWS, WROWS), WROWS)
    mate_rows = pl.ds(pl.multiple_of((1 - x_lo) * WROWS, WROWS), WROWS)
    added_rows = pl.ds(pl.multiple_of(x_lo * SPLIT + (1 - x_lo) * WROWS, 16), REST - WROWS)

    def yf(dy, lanes=slice(None)):
        return w.at[block(dy, 0), :, pl.ds(late, SPLIT), lanes]

    def yf_plane(dz, piece, lanes=slice(None)):
        return w.at[((z - dz + NZ) % NZ) * NY + piece, :, pl.ds(late, SPLIT), lanes]

    def zf(dy, dz, lanes=slice(None), rows=pl.ds(early, REST)):
        return w.at[block(dy, dz), :, rows, lanes]

    def tk(dx, cc, start=0, rows=TOK):
        xx = (x - dx + NX) % NX
        row = pl.multiple_of(HALO + (xx % 2) * TOK + start, 16)
        col = pl.multiple_of(((xx // 2) * 2 + cc) * FEAT, FEAT)
        return tok.at[pl.ds(row, rows), pl.ds(col, FEAT)]

    HALF = TOK // 2

    mine = pl.ds(pl.multiple_of(x_lo * WIDTH, WIDTH), WIDTH)
    theirs = pl.ds(pl.multiple_of((1 - x_lo) * WIDTH, WIDTH), WIDTH)
    own_w = local(-1, weights.at[:, :, mine], w.at[blk, :, own_rows])
    own_filt = local(-2, filt_hbm, filt)
    own_tok = local(-3, tokens, tk(0, core))
    tables_in = [
        local(name, src, dst)
        for name, src, dst in (
            (-5, first_hbm, first), (-6, last_hbm, last), (-7, ahead_hbm, ahead), (-8, back_hbm, back),
            (-9, twist_hbm, twist), (-10, taps_hbm, taps), (-11, skip_hbm, skip),
        )
    ]

    def rows8(index):
        return pl.ds(pl.multiple_of(index * 8, 8), 8)

    def rows16(index):
        return pl.ds(pl.multiple_of(index * 16, 16), 16)

    own_filt.wait()
    for i in range(4):
        for j in range(2):
            filt_t[i % 2, pl.ds((i // 2) * WIDTH + j, SIDE, stride=2), :] = filt[
                j * 128 : (j + 1) * 128, i * 128 : (i + 1) * 128
            ].T
    pltpu.make_async_copy(filt_t.at[:, rows8(x_lo * BLOCKS + blk)], filt_in.at[:, rows8(seq)], many.at[1]).start()
    own_w.wait()
    pl.semaphore_wait(barrier, SEQ + 1)

    copies = {}

    def plan(name, src, device, after, comes, dst=None):
        copies[name] = (src, src if dst is None else dst, device, after, comes)

    def zf_parts(dz):
        if dz == 0:
            return [key(SWAP)]
        if abs(dz) == 1:
            return [key(ZF_OWN, dz), key(ZF_ADDED, dz)]
        return [key(ZF, 4), key(ZF, -4)] if dz == 4 else [key(ZF, dz)]

    everything = slice(None)
    plan(key(SWAP), weights.at[:, :, theirs], mate, [], w.at[blk, :, mate_rows], w.at[blk, :, own_rows])
    for sign, lanes in ((1, LO), (-1, HI)):
        for own, own_y, rows, after in (
            (ZF_OWN, ZFY_OWN, own_rows, []), (ZF_ADDED, ZFY_ADDED, added_rows, [key(SWAP)]),
        ):
            ref = zf(0, 0, rows=rows)
            plan(key(own, sign), ref, at_yz(0, sign), after, zf(0, sign, rows=rows))
            plan(key(own_y, sign), ref, at_yz(sign, 0), after, zf(sign, 0, rows=rows))
        for dz in (2, 3, 4):
            part = lanes if dz == 4 else everything
            far = sign * dz
            plan(key(ZF, far), zf(0, far - sign, part), at_yz(0, sign), zf_parts(far - sign), zf(0, far, part))
        for dz in range(-3, 5):
            after = [key(ZFY_OWN, sign), key(ZFY_ADDED, sign)]
            if dz != 0:
                after = [key(ZFY, dz, sign)]
                plan(after[0], zf(0, dz), at_yz(sign, 0), zf_parts(dz), zf(sign, dz))
            plan(key(ZFY, dz, 2 * sign), zf(sign, dz, lanes), at_yz(sign, 0), after, zf(2 * sign, dz, lanes))
        plan(key(YF, sign), yf(0), at_yz(sign, 0), [key(SWAP)], yf(sign))
        plan(key(YF, 2 * sign), yf(sign, lanes), at_yz(sign, 0), [key(YF, sign)], yf(2 * sign, lanes))
        for dz in (1, 2, 3, 4):
            part = lanes if dz == 4 else everything
            for piece in range(NY):
                near = sign * (dz - 1)
                after = [key(PLANE, near, piece)] if dz > 1 else [key(YF, by) for by in AROUND]
                plan(
                    key(PLANE, sign * dz, piece), yf_plane(near, piece, part), at_yz(0, sign), after,
                    yf_plane(sign * dz, piece, part),
                )
        start = 0 if sign == 1 else HALF
        plan(key(TOKEN, sign), tokens, at_x(sign), [], tk(sign, core), tk(0, core))
        plan(
            key(TOKEN, 2 * sign), tk(sign, core, start, HALF), at_x(sign), [key(TOKEN, sign)],
            tk(2, core, start, HALF),
        )
        plan(key(CORE, sign), tk(sign, core), twin, [key(TOKEN, sign)], tk(sign, 1 - core))
        plan(
            key(CORE, 2 * sign), tk(2, core, start, HALF), twin, [key(TOKEN, 2 * sign)],
            tk(2, 1 - core, start, HALF),
        )
    plan(key(CORE), tokens, twin, [], tk(0, 1 - core), tk(0, core))
    after = (blk + 1) % BLOCKS
    all_tok = [key(kind, by) for kind in (TOKEN, CORE) for by in AROUND] + [key(CORE)]
    halo = tok.at[pl.ds(0, HALO)]
    plan(key(LAST_ROWS), tok.at[pl.ds(POS, HALO)], {"seq": after * 2 + x_lo}, all_tok, halo, halo)

    here = set()

    def need(names):
        for name in names:
            if name not in here:
                arrived(name, copies[name][4])
                here.add(name)

    def plane_parts(dz):
        parts = zf_parts(dz) + [key(ZFY, dz, by) for by in (2, -2)]
        if dz == 0:
            near = [key(kind, by) for kind in (ZFY_OWN, ZFY_ADDED) for by in (1, -1)]
            return parts + near + [key(YF, by) for by in AROUND]
        ends = (4, -4) if dz == 4 else (dz,)
        parts += [key(ZFY, dz, by) for by in (1, -1)]
        return parts + [key(PLANE, end, piece) for end in ends for piece in range(NY)]

    def project(dz, fresh=False):
        plane = (z - dz + NZ) % NZ

        def part(i, _):
            cols = pl.ds(pl.multiple_of(i * 256, 256), 256)
            term = mm(
                tok[:, pl.ds(pl.multiple_of(plane * 512, 512), 512)],
                w[pl.ds(plane * NY, NY), i].reshape(512, 256),
            )
            acc[:, cols] = term if fresh else acc[:, cols] + term
            return 0

        lax.fori_loop(0, 3, part, 0)

    def give_filter(part):
        def give(i, _):
            peer = (seq + SPREAD * i) % SEQ
            pltpu.make_async_remote_copy(
                src_ref=filt_t.at[:, rows8((peer % 2) * BLOCKS + peer // 2)], dst_ref=filt_in.at[:, rows8(seq)],
                send_sem=many.at[0], recv_sem=many.at[1], device_id={"seq": peer}, device_id_type=MESH,
            ).start()
            return 0

        lax.fori_loop(1 + 9 * part, 10 + 9 * part, give, 0)

    def transform(load, pair):
        columns = jnp.concatenate([load(2 * pair), load(2 * pair + 1)], axis=1)
        high, low = halves(columns)
        turned = mm(first[...], jnp.concatenate([high, low, high], axis=0))
        cos, sin = twist[0], twist[1]
        rows = []
        for i in range(2):
            real = turned[:SIDE, i * SIDE : (i + 1) * SIDE]
            imag = turned[SIDE:, i * SIDE : (i + 1) * SIDE]
            rows.append(jnp.concatenate([real * cos + imag * sin, imag * cos - real * sin], axis=1))
        return right_apply(jnp.concatenate(rows, axis=0), ahead)

    def load_filter(c):
        return jnp.concatenate(
            [
                filt_in[c // 4, pl.ds(8 * (j // 2) + 2 * (c % 4) + j % 2, BLOCKS, stride=16), :]
                for j in range(4)
            ],
            axis=0,
        )

    def load_gate(c):
        return jnp.concatenate(
            [gate_in[c // 4, pl.ds(4 * (c % 4) + j, BLOCKS, stride=16), :] for j in range(4)], axis=0
        )

    def respond():
        for copy in tables_in:
            copy.wait()
        whole = filt_in.at[:, pl.ds(0, ROWS)]
        pltpu.make_async_copy(whole, whole, many.at[1]).wait()
        for pair in range(OWN // 2):
            spec[pair * 256 : (pair + 1) * 256, :] = transform(load_filter, pair)

    fresh = True
    for step in STEPS:
        kind, number = step // 100, step // 10 % 10 - 4
        if step in copies:
            src, dst, device, after, _ = copies[step]
            need(after)
            if kind == LAST_ROWS:
                own_tok.wait()
            go(step, src, dst, device)
        elif kind == PROJECT:
            need([key(LAST_ROWS)] if fresh else [])
            need(plane_parts(number))
            project(number, fresh)
            fresh = False
        elif kind == GIVE:
            give_filter(number + 4)
        else:
            respond()
    assert here == set(copies)

    acc[8:16, :] = jnp.where(blk == 0, 0.0, acc[8:16, :])
    taps_col = pl.ds(pl.multiple_of(x_lo * WIDTH, WIDTH), WIDTH)
    tap = [[taps[j, pl.ds(s, 1), taps_col] for s in range(3)] for j in range(TAPS)]

    def give_gate(half):
        def give(i, _):
            peer = (blk + SPREAD * i) % BLOCKS
            pltpu.make_async_remote_copy(
                src_ref=gate_t.at[half, rows16(peer)], dst_ref=gate_in.at[half, rows16(blk)],
                send_sem=many.at[2], recv_sem=many.at[3 + half], device_id={"seq": peer * 2 + x_lo},
                device_id_type=MESH,
            ).start()
            return 0

        lax.fori_loop(1, BLOCKS, give, 0)
        pltpu.make_async_copy(gate_t.at[half, rows16(blk)], gate_in.at[half, rows16(blk)], many.at[3 + half]).start()

    for half, gated in ((0, True), (0, False), (1, False), (1, True)):
        lanes = slice(half * SIDE, (half + 1) * SIDE)
        for row in range(4):

            def short(s):
                total = None
                for j in range(TAPS):
                    start = HALO - j + row * SIDE
                    cols = slice(s * WIDTH + half * SIDE, s * WIDTH + (half + 1) * SIDE)
                    term = tap[j][s][:, lanes] * acc[start : start + SIDE, cols]
                    total = term if total is None else total + term
                return total

            if gated:
                gate_t[half, pl.ds(row, SIDE, stride=4), :] = (short(1) * short(2)).T
            else:
                outer_t[row, lanes, :] = short(0).T
        if gated:
            give_gate(half)
    go(-4, outer_t.at[pl.ds(2 * (1 - x_lo), 2)], outer.at[:, mine], mate)
    own_outer = local(-12, outer_t.at[pl.ds(2 * x_lo, 2)], outer.at[:, mine])

    def all_sent(number, ref, rows):
        sent = ref.at[:, pl.ds(rows, ROWS - rows)]
        pltpu.make_async_copy(sent, sent, many.at[number]).wait()

    for copy in started[:-1]:
        copy.wait_send()
    all_sent(0, filt_t, 8)

    def convolve(pair):
        spectrum = transform(load_gate, pair)
        response = spec[pair * 256 : (pair + 1) * 256, :]
        sr, si = spectrum[:, :SIDE], spectrum[:, SIDE:]
        rr, ri = response[:, :SIDE], response[:, SIDE:]
        product = jnp.concatenate([sr * rr - si * ri, sr * ri + si * rr], axis=1)
        inverse = right_apply(product, back)
        cos, sin = twist[0], twist[1]
        cols = []
        for i in range(2):
            real = inverse[i * SIDE : (i + 1) * SIDE, :SIDE]
            imag = inverse[i * SIDE : (i + 1) * SIDE, SIDE:]
            cols.append(jnp.concatenate([real * cos - imag * sin, imag * cos + real * sin], axis=0))
        high, low = halves(jnp.concatenate(cols, axis=1))
        result = mm(last[...], jnp.concatenate([high, low, high], axis=0))
        for i in range(2):
            c = 2 * pair + i
            gain = skip[x_lo * WIDTH + (c // 4) * SIDE + blk * 4 + c % 4]
            total = result[:, i * SIDE : (i + 1) * SIDE] + gain * load_gate(c)
            for j in range(4):
                place = pl.ds(8 * (j // 2) + 2 * (c % 4) + j % 2, BLOCKS, stride=16)
                y_out[c // 4, place, :] = total[j * BLOCKS : (j + 1) * BLOCKS, :]

    def give_y(half):
        here8 = rows8(x_lo * BLOCKS + blk)

        def give(i, _):
            peer = (seq + SPREAD * i) % SEQ
            pltpu.make_async_remote_copy(
                src_ref=y_out.at[half, rows8(peer)], dst_ref=y_in.at[half, here8],
                send_sem=many.at[5], recv_sem=many.at[6 + half], device_id={"seq": peer}, device_id_type=MESH,
            ).start()
            return 0

        lax.fori_loop(1, SEQ, give, 0)
        pltpu.make_async_copy(y_out.at[half, rows8(seq)], y_in.at[half, here8], many.at[6 + half]).start()

    for half in range(2):
        whole = gate_in.at[half, pl.ds(0, ROWS)]
        pltpu.make_async_copy(whole, whole, many.at[3 + half]).wait()
        convolve(2 * half)
        convolve(2 * half + 1)
        give_y(half)

    started[-1].wait_send()
    all_sent(2, gate_t, 16)
    own_outer.wait()
    arrived(-4, outer.at[:, theirs])
    for half in range(2):
        whole = y_in.at[half, pl.ds(0, ROWS)]
        pltpu.make_async_copy(whole, whole, many.at[6 + half]).wait()
        for side in range(2):
            cols = slice(side * WIDTH + half * SIDE, side * WIDTH + (half + 1) * SIDE)
            for j in range(2):
                value = outer[j, cols, :] * y_in[half, pl.ds(side * WIDTH + j, SIDE, stride=2), :]
                out[j * SIDE : (j + 1) * SIDE, cols] = value.T.astype(BF16)

    all_sent(5, y_out, 8)


SLOTS = 112


def local(tokens, in_weight, short_filter, long_filter, skip_gain):
    width = skip_gain.shape[0]
    weights = in_weight.transpose(1, 0, 2)
    held = tables()
    vmem = pl.BlockSpec(memory_space=pltpu.VMEM)
    anywhere = pl.BlockSpec(memory_space=pl.ANY)
    out = pl.pallas_call(
        kernel,
        out_shape=jax.ShapeDtypeStruct((TOK, width), BF16),
        in_specs=[anywhere] * (5 + len(held)),
        out_specs=vmem,
        scratch_shapes=[
            pltpu.VMEM((TOK, width), F32),
            pltpu.VMEM((TAPS, 3, width), F32),
            pltpu.SMEM((width,), F32),
            *[pltpu.VMEM(table.shape, table.dtype) for table in held],
            pltpu.VMEM((BLOCKS, 3, 2 * WROWS, WIDTH), BF16),
            pltpu.VMEM((HALO + POS, CH * FEAT), BF16),
            pltpu.VMEM((HALO + POS, COLS), F32),
            pltpu.VMEM((2, ROWS + 16, SIDE), F32),
            pltpu.VMEM((2, ROWS + 16, SIDE), F32),
            pltpu.VMEM((2, ROWS + 16, SIDE), F32),
            pltpu.VMEM((2, ROWS + 16, SIDE), F32),
            pltpu.VMEM((4, WIDTH, SIDE), F32),
            pltpu.VMEM((2, 2 * WIDTH, SIDE), F32),
            pltpu.VMEM((2, ROWS + 16, SIDE), F32),
            pltpu.VMEM((2, ROWS + 16, SIDE), F32),
            pltpu.VMEM((OWN * SIDE, 2 * SIDE), F32),
            pltpu.SemaphoreType.DMA((SLOTS,)),
            pltpu.SemaphoreType.DMA((SLOTS,)),
            pltpu.SemaphoreType.DMA((8,)),
        ],
        compiler_params=pltpu.CompilerParams(
            collective_id=0, has_side_effects=True, vmem_limit_bytes=60 * 1024 * 1024
        ),
    )(tokens, weights, long_filter, short_filter, skip_gain, *held)
    return out


def solution(mesh):
    placed = (P("seq", "ch"), P("seq", None, "ch"), P(None, None, "ch"), P("seq", "ch"), P("ch"))
    return jax.shard_map(
        local, mesh=mesh, in_specs=placed, out_specs=P("seq", "ch"), check_vma=False
    )
```

```python
import math

import jax
import jax.numpy as jnp
import ml_dtypes
import numpy as np
from jax import lax
from jax.experimental import pallas as pl
from jax.experimental.pallas import tpu as pltpu
from jax.sharding import PartitionSpec as P

MESH = pl.DeviceIdType.MESH
BF16, F32 = jnp.bfloat16, jnp.float32

NZ, NY, NX = 8, 4, 4
AROUND = (1, -1, 2, -2)
SEQ, CH = 64, 4
BLOCKS = NZ * NY
TOK = 256
POS = 2 * TOK
FEAT = 1024
HALO = 16
TAPS = 3
WIDTH = 256
COLS = 3 * WIDTH
OWN = 8
WROWS = 64
SPLIT = 48
SIDE = 128
LENGTH = SIDE * SIDE
SPREAD = 27
ROWS = 512
LO, HI = pl.ds(0, WIDTH // 2), pl.ds(WIDTH // 2, WIDTH // 2)
REST = 2 * WROWS - SPLIT


SWAP, ZF_OWN, ZF_ADDED, ZF, ZFY_OWN, ZFY_ADDED, ZFY, YF, PLANE, TOKEN, CORE, LAST_ROWS, GIVE, RESPOND, PROJECT = (*range(12), 13, 14, 15)


def key(kind, first=0, second=0):
    return 100 * kind + 10 * (first + 4) + second + 4


STEPS = (
    44, 454, 434, 134, 154, 1044, 954, 934, 1304, 1314, 534, 554, 254, 734, 754, 234, 1324, 642, 646, 655,
    653, 364, 633, 635, 324, 1334, 724, 764, 1344, 1354, 1054, 964, 856, 834, 835, 836, 857, 855, 837, 854, 1034,
    924, 1364, 665, 663, 625, 623, 314, 374, 656, 632, 652, 636, 1064, 1024, 1144, 866, 824, 825, 826, 867, 865,
    827, 864, 1444, 662, 626, 622, 666, 615, 613, 304, 675, 673, 384, 1544, 1554, 1534, 876, 814, 815, 877, 875,
    1564, 817, 874, 816, 685, 683, 1524, 612, 672, 616, 676, 886, 804, 805, 887, 885, 884, 806, 807, 682, 686, 1514,
    1574, 1584,
)


def split_table(table):
    high = table.astype(ml_dtypes.bfloat16)
    low = (table - high.astype(np.float64)).astype(ml_dtypes.bfloat16)
    return high, low


def tables():
    slot = np.arange(SIDE)
    n1 = 4 * (slot % BLOCKS) + slot // BLOCKS
    k = np.arange(SIDE)
    outer = 2.0 * math.pi * ((np.outer(4 * k + 1, n1)) % 512) / 512.0
    first = np.concatenate([np.cos(outer), -np.sin(outer)], axis=0)
    last = np.concatenate([np.cos(outer).T, -np.sin(outer).T], axis=1) / LENGTH
    inner = 2.0 * math.pi * (np.outer(k, k) % SIDE) / SIDE
    cos, sin = np.cos(inner), np.sin(inner)
    ahead = np.block([[cos, -sin], [sin, cos]])
    back = np.block([[cos, sin], [-sin, cos]])
    twist = 2.0 * math.pi * np.outer(4 * k + 1, k) / (4.0 * LENGTH)
    fh, fl = split_table(first)
    lh, ll = split_table(last)
    return (
        np.concatenate([fh, fh, fl], axis=1),
        np.concatenate([lh, lh, ll], axis=1),
        np.stack(split_table(ahead)),
        np.stack(split_table(back)),
        np.stack([np.cos(twist), np.sin(twist)]).astype(np.float32),
    )


def halves(values):
    high = values.astype(BF16)
    return high, (values - high.astype(F32)).astype(BF16)


def mm(a, b):
    return jnp.dot(a, b, preferred_element_type=F32)


def right_apply(values, table):
    high, low = halves(values)
    return mm(high, table[0]) + mm(low, table[0]) + mm(high, table[1])


def kernel(
    tokens, weights, filt_hbm, taps_hbm, skip_hbm, first_hbm, last_hbm, ahead_hbm, back_hbm, twist_hbm,
    out,
    filt, taps, skip, first, last, ahead, back, twist,
    w, tok, acc, filt_t, filt_in, gate_t, gate_in, outer_t, outer, y_out, y_in, spec,
    send, recv, many,
):
    seq = lax.axis_index("seq")
    ch = lax.axis_index("ch")
    x_lo, blk = seq % 2, seq // 2
    y, z = blk % NY, blk // NY
    x_hi, core = ch // 2, ch % 2
    x = x_hi * 2 + x_lo

    def seq_of(zz, yy, xx):
        return (zz * NY + yy) * 2 + xx

    def at_yz(dy, dz):
        return {"seq": seq_of((z + dz + NZ) % NZ, (y + dy + NY) % NY, x_lo)}

    def at_x(dx):
        xx = (x + dx + NX) % NX
        return {"seq": seq_of(z, y, xx % 2), "ch": (xx // 2) * 2 + core}

    twin = {"ch": x_hi * 2 + 1 - core}
    mate = {"seq": seq_of(z, y, 1 - x_lo)}

    barrier = pltpu.get_barrier_semaphore()

    def greet(i, _):
        pl.semaphore_signal(barrier, inc=1, device_id={"seq": (seq + i) % SEQ}, device_id_type=MESH)
        return 0

    lax.fori_loop(1, SEQ, greet, 0)
    pl.semaphore_signal(barrier, inc=1, device_id=twin, device_id_type=MESH)
    pl.semaphore_signal(barrier, inc=1, device_id=at_x(3 + 2 * x_lo), device_id_type=MESH)

    started = []
    slots = {}

    def slot(name):
        return slots.setdefault(name, len(slots))

    def go(name, src, dst, device):
        copy = pltpu.make_async_remote_copy(
            src_ref=src, dst_ref=dst, send_sem=send.at[slot(name)], recv_sem=recv.at[slot(name)],
            device_id=device, device_id_type=MESH,
        )
        copy.start()
        started.append(copy)

    def arrived(name, dst):
        pltpu.make_async_copy(dst, dst, recv.at[slot(name)]).wait()

    def local(name, src, dst):
        copy = pltpu.make_async_copy(src, dst, recv.at[slot(name)])
        copy.start()
        return copy

    def block(dy, dz):
        return ((z - dz + NZ) % NZ) * NY + (y - dy + NY) % NY

    early = pl.multiple_of(x_lo * SPLIT, 16)
    late = pl.multiple_of((1 - x_lo) * REST, 16)
    own_rows = pl.ds(pl.multiple_of(x_lo * WROWS, WROWS), WROWS)
    mate_rows = pl.ds(pl.multiple_of((1 - x_lo) * WROWS, WROWS), WROWS)
    added_rows = pl.ds(pl.multiple_of(x_lo * SPLIT + (1 - x_lo) * WROWS, 16), REST - WROWS)

    def yf(dy, lanes=slice(None)):
        return w.at[block(dy, 0), :, pl.ds(late, SPLIT), lanes]

    def yf_plane(dz, piece, lanes=slice(None)):
        return w.at[((z - dz + NZ) % NZ) * NY + piece, :, pl.ds(late, SPLIT), lanes]

    def zf(dy, dz, lanes=slice(None), rows=pl.ds(early, REST)):
        return w.at[block(dy, dz), :, rows, lanes]

    def tk(dx, cc, start=0, rows=TOK):
        xx = (x - dx + NX) % NX
        row = pl.multiple_of(HALO + (xx % 2) * TOK + start, 16)
        col = pl.multiple_of(((xx // 2) * 2 + cc) * FEAT, FEAT)
        return tok.at[pl.ds(row, rows), pl.ds(col, FEAT)]

    HALF = TOK // 2

    mine = pl.ds(pl.multiple_of(x_lo * WIDTH, WIDTH), WIDTH)
    theirs = pl.ds(pl.multiple_of((1 - x_lo) * WIDTH, WIDTH), WIDTH)
    own_w = local(-1, weights.at[:, :, mine], w.at[blk, :, own_rows])
    own_filt = local(-2, filt_hbm, filt)
    own_tok = local(-3, tokens, tk(0, core))
    tables_in = [
        local(name, src, dst)
        for name, src, dst in (
            (-5, first_hbm, first), (-6, last_hbm, last), (-7, ahead_hbm, ahead), (-8, back_hbm, back),
            (-9, twist_hbm, twist), (-10, taps_hbm, taps), (-11, skip_hbm, skip),
        )
    ]

    def rows8(index):
        return pl.ds(pl.multiple_of(index * 8, 8), 8)

    def rows16(index):
        return pl.ds(pl.multiple_of(index * 16, 16), 16)

    own_filt.wait()
    for i in range(4):
        for j in range(2):
            filt_t[i % 2, pl.ds((i // 2) * WIDTH + j, SIDE, stride=2), :] = filt[
                j * 128 : (j + 1) * 128, i * 128 : (i + 1) * 128
            ].T
    pltpu.make_async_copy(filt_t.at[:, rows8(x_lo * BLOCKS + blk)], filt_in.at[:, rows8(seq)], many.at[1]).start()
    own_w.wait()
    pl.semaphore_wait(barrier, SEQ + 1)

    copies = {}

    def plan(name, src, device, after, comes, dst=None):
        copies[name] = (src, src if dst is None else dst, device, after, comes)

    def zf_parts(dz):
        if dz == 0:
            return [key(SWAP)]
        if abs(dz) == 1:
            return [key(ZF_OWN, dz), key(ZF_ADDED, dz)]
        return [key(ZF, 4), key(ZF, -4)] if dz == 4 else [key(ZF, dz)]

    everything = slice(None)
    plan(key(SWAP), weights.at[:, :, theirs], mate, [], w.at[blk, :, mate_rows], w.at[blk, :, own_rows])
    for sign, lanes in ((1, LO), (-1, HI)):
        for own, own_y, rows, after in (
            (ZF_OWN, ZFY_OWN, own_rows, []), (ZF_ADDED, ZFY_ADDED, added_rows, [key(SWAP)]),
        ):
            ref = zf(0, 0, rows=rows)
            plan(key(own, sign), ref, at_yz(0, sign), after, zf(0, sign, rows=rows))
            plan(key(own_y, sign), ref, at_yz(sign, 0), after, zf(sign, 0, rows=rows))
        for dz in (2, 3, 4):
            part = lanes if dz == 4 else everything
            far = sign * dz
            plan(key(ZF, far), zf(0, far - sign, part), at_yz(0, sign), zf_parts(far - sign), zf(0, far, part))
        for dz in range(-3, 5):
            after = [key(ZFY_OWN, sign), key(ZFY_ADDED, sign)]
            if dz != 0:
                after = [key(ZFY, dz, sign)]
                plan(after[0], zf(0, dz), at_yz(sign, 0), zf_parts(dz), zf(sign, dz))
            plan(key(ZFY, dz, 2 * sign), zf(sign, dz, lanes), at_yz(sign, 0), after, zf(2 * sign, dz, lanes))
        plan(key(YF, sign), yf(0), at_yz(sign, 0), [key(SWAP)], yf(sign))
        plan(key(YF, 2 * sign), yf(sign, lanes), at_yz(sign, 0), [key(YF, sign)], yf(2 * sign, lanes))
        for dz in (1, 2, 3, 4):
            part = lanes if dz == 4 else everything
            for piece in range(NY):
                near = sign * (dz - 1)
                after = [key(PLANE, near, piece)] if dz > 1 else [key(YF, by) for by in AROUND]
                plan(
                    key(PLANE, sign * dz, piece), yf_plane(near, piece, part), at_yz(0, sign), after,
                    yf_plane(sign * dz, piece, part),
                )
        start = 0 if sign == 1 else HALF
        plan(key(TOKEN, sign), tokens, at_x(sign), [], tk(sign, core), tk(0, core))
        plan(
            key(TOKEN, 2 * sign), tk(sign, core, start, HALF), at_x(sign), [key(TOKEN, sign)],
            tk(2, core, start, HALF),
        )
        plan(key(CORE, sign), tk(sign, core), twin, [key(TOKEN, sign)], tk(sign, 1 - core))
        plan(
            key(CORE, 2 * sign), tk(2, core, start, HALF), twin, [key(TOKEN, 2 * sign)],
            tk(2, 1 - core, start, HALF),
        )
    plan(key(CORE), tokens, twin, [], tk(0, 1 - core), tk(0, core))
    after = (blk + 1) % BLOCKS
    all_tok = [key(kind, by) for kind in (TOKEN, CORE) for by in AROUND] + [key(CORE)]
    halo = tok.at[pl.ds(0, HALO)]
    plan(key(LAST_ROWS), tok.at[pl.ds(POS, HALO)], {"seq": after * 2 + x_lo}, all_tok, halo, halo)

    here = set()

    def need(names):
        for name in names:
            if name not in here:
                arrived(name, copies[name][4])
                here.add(name)

    def plane_parts(dz):
        parts = zf_parts(dz) + [key(ZFY, dz, by) for by in (2, -2)]
        if dz == 0:
            near = [key(kind, by) for kind in (ZFY_OWN, ZFY_ADDED) for by in (1, -1)]
            return parts + near + [key(YF, by) for by in AROUND]
        ends = (4, -4) if dz == 4 else (dz,)
        parts += [key(ZFY, dz, by) for by in (1, -1)]
        return parts + [key(PLANE, end, piece) for end in ends for piece in range(NY)]

    def project(dz, fresh=False):
        plane = (z - dz + NZ) % NZ

        def part(i, _):
            cols = pl.ds(pl.multiple_of(i * 256, 256), 256)
            term = mm(
                tok[:, pl.ds(pl.multiple_of(plane * 512, 512), 512)],
                w[pl.ds(plane * NY, NY), i].reshape(512, 256),
            )
            acc[:, cols] = term if fresh else acc[:, cols] + term
            return 0

        lax.fori_loop(0, 3, part, 0)

    def give_filter(part):
        def give(i, _):
            peer = (seq + SPREAD * i) % SEQ
            pltpu.make_async_remote_copy(
                src_ref=filt_t.at[:, rows8((peer % 2) * BLOCKS + peer // 2)], dst_ref=filt_in.at[:, rows8(seq)],
                send_sem=many.at[0], recv_sem=many.at[1], device_id={"seq": peer}, device_id_type=MESH,
            ).start()
            return 0

        lax.fori_loop(1 + 9 * part, 10 + 9 * part, give, 0)

    def transform(load, pair):
        columns = jnp.concatenate([load(2 * pair), load(2 * pair + 1)], axis=1)
        high, low = halves(columns)
        turned = mm(first[...], jnp.concatenate([high, low, high], axis=0))
        cos, sin = twist[0], twist[1]
        rows = []
        for i in range(2):
            real = turned[:SIDE, i * SIDE : (i + 1) * SIDE]
            imag = turned[SIDE:, i * SIDE : (i + 1) * SIDE]
            rows.append(jnp.concatenate([real * cos + imag * sin, imag * cos - real * sin], axis=1))
        return right_apply(jnp.concatenate(rows, axis=0), ahead)

    def load_filter(c):
        return jnp.concatenate(
            [
                filt_in[c // 4, pl.ds(8 * (j // 2) + 2 * (c % 4) + j % 2, BLOCKS, stride=16), :]
                for j in range(4)
            ],
            axis=0,
        )

    def load_gate(c):
        return jnp.concatenate(
            [gate_in[c // 4, pl.ds(4 * (c % 4) + j, BLOCKS, stride=16), :] for j in range(4)], axis=0
        )

    def respond():
        for copy in tables_in:
            copy.wait()
        whole = filt_in.at[:, pl.ds(0, ROWS)]
        pltpu.make_async_copy(whole, whole, many.at[1]).wait()
        for pair in range(OWN // 2):
            spec[pair * 256 : (pair + 1) * 256, :] = transform(load_filter, pair)

    fresh = True
    for step in STEPS:
        kind, number = step // 100, step // 10 % 10 - 4
        if step in copies:
            src, dst, device, after, _ = copies[step]
            need(after)
            if kind == LAST_ROWS:
                own_tok.wait()
            go(step, src, dst, device)
        elif kind == PROJECT:
            need([key(LAST_ROWS)] if fresh else [])
            need(plane_parts(number))
            project(number, fresh)
            fresh = False
        elif kind == GIVE:
            give_filter(number + 4)
        else:
            respond()
    assert here == set(copies)

    acc[8:16, :] = jnp.where(blk == 0, 0.0, acc[8:16, :])
    taps_col = pl.ds(pl.multiple_of(x_lo * WIDTH, WIDTH), WIDTH)
    tap = [[taps[j, pl.ds(s, 1), taps_col] for s in range(3)] for j in range(TAPS)]

    def give_gate(half):
        def give(i, _):
            peer = (blk + SPREAD * i) % BLOCKS
            pltpu.make_async_remote_copy(
                src_ref=gate_t.at[half, rows16(peer)], dst_ref=gate_in.at[half, rows16(blk)],
                send_sem=many.at[2], recv_sem=many.at[3 + half], device_id={"seq": peer * 2 + x_lo},
                device_id_type=MESH,
            ).start()
            return 0

        lax.fori_loop(1, BLOCKS, give, 0)
        pltpu.make_async_copy(gate_t.at[half, rows16(blk)], gate_in.at[half, rows16(blk)], many.at[3 + half]).start()

    for stage in range(4):
        half = stage % 2
        lanes = slice(half * SIDE, (half + 1) * SIDE)
        for row in range(4):

            def short(s):
                total = None
                for j in range(TAPS):
                    start = HALO - j + row * SIDE
                    cols = slice(s * WIDTH + half * SIDE, s * WIDTH + (half + 1) * SIDE)
                    term = tap[j][s][:, lanes] * acc[start : start + SIDE, cols]
                    total = term if total is None else total + term
                return total

            if stage < 2:
                gate_t[half, pl.ds(row, SIDE, stride=4), :] = (short(1) * short(2)).T
            else:
                outer_t[row, lanes, :] = short(0).T
        if stage < 2:
            give_gate(half)
    go(-4, outer_t.at[pl.ds(2 * (1 - x_lo), 2)], outer.at[:, mine], mate)
    own_outer = local(-12, outer_t.at[pl.ds(2 * x_lo, 2)], outer.at[:, mine])

    def all_sent(number, ref, rows):
        sent = ref.at[:, pl.ds(rows, ROWS - rows)]
        pltpu.make_async_copy(sent, sent, many.at[number]).wait()

    for copy in started[:-1]:
        copy.wait_send()
    all_sent(0, filt_t, 8)

    def convolve(pair):
        spectrum = transform(load_gate, pair)
        response = spec[pair * 256 : (pair + 1) * 256, :]
        sr, si = spectrum[:, :SIDE], spectrum[:, SIDE:]
        rr, ri = response[:, :SIDE], response[:, SIDE:]
        product = jnp.concatenate([sr * rr - si * ri, sr * ri + si * rr], axis=1)
        inverse = right_apply(product, back)
        cos, sin = twist[0], twist[1]
        cols = []
        for i in range(2):
            real = inverse[i * SIDE : (i + 1) * SIDE, :SIDE]
            imag = inverse[i * SIDE : (i + 1) * SIDE, SIDE:]
            cols.append(jnp.concatenate([real * cos - imag * sin, imag * cos + real * sin], axis=0))
        high, low = halves(jnp.concatenate(cols, axis=1))
        result = mm(last[...], jnp.concatenate([high, low, high], axis=0))
        for i in range(2):
            c = 2 * pair + i
            gain = skip[x_lo * WIDTH + (c // 4) * SIDE + blk * 4 + c % 4]
            total = result[:, i * SIDE : (i + 1) * SIDE] + gain * load_gate(c)
            for j in range(4):
                place = pl.ds(8 * (j // 2) + 2 * (c % 4) + j % 2, BLOCKS, stride=16)
                y_out[c // 4, place, :] = total[j * BLOCKS : (j + 1) * BLOCKS, :]

    def give_y(half):
        here8 = rows8(x_lo * BLOCKS + blk)

        def give(i, _):
            peer = (seq + SPREAD * i) % SEQ
            pltpu.make_async_remote_copy(
                src_ref=y_out.at[half, rows8(peer)], dst_ref=y_in.at[half, here8],
                send_sem=many.at[5], recv_sem=many.at[6 + half], device_id={"seq": peer}, device_id_type=MESH,
            ).start()
            return 0

        lax.fori_loop(1, SEQ, give, 0)
        pltpu.make_async_copy(y_out.at[half, rows8(seq)], y_in.at[half, here8], many.at[6 + half]).start()

    for half in range(2):
        whole = gate_in.at[half, pl.ds(0, ROWS)]
        pltpu.make_async_copy(whole, whole, many.at[3 + half]).wait()
        convolve(2 * half)
        convolve(2 * half + 1)
        give_y(half)

    started[-1].wait_send()
    all_sent(2, gate_t, 16)
    own_outer.wait()
    arrived(-4, outer.at[:, theirs])
    for half in range(2):
        whole = y_in.at[half, pl.ds(0, ROWS)]
        pltpu.make_async_copy(whole, whole, many.at[6 + half]).wait()
        for side in range(2):
            cols = slice(side * WIDTH + half * SIDE, side * WIDTH + (half + 1) * SIDE)
            for j in range(2):
                value = outer[j, cols, :] * y_in[half, pl.ds(side * WIDTH + j, SIDE, stride=2), :]
                out[j * SIDE : (j + 1) * SIDE, cols] = value.T

    all_sent(5, y_out, 8)


SLOTS = 112


def local(tokens, in_weight, short_filter, long_filter, skip_gain):
    width = skip_gain.shape[0]
    weights = in_weight.transpose(1, 0, 2)
    held = tables()
    vmem = pl.BlockSpec(memory_space=pltpu.VMEM)
    anywhere = pl.BlockSpec(memory_space=pl.ANY)
    out = pl.pallas_call(
        kernel,
        out_shape=jax.ShapeDtypeStruct((TOK, width), F32),
        in_specs=[anywhere] * (5 + len(held)),
        out_specs=vmem,
        scratch_shapes=[
            pltpu.VMEM((TOK, width), F32),
            pltpu.VMEM((TAPS, 3, width), F32),
            pltpu.SMEM((width,), F32),
            *[pltpu.VMEM(table.shape, table.dtype) for table in held],
            pltpu.VMEM((BLOCKS, 3, 2 * WROWS, WIDTH), BF16),
            pltpu.VMEM((HALO + POS, CH * FEAT), BF16),
            pltpu.VMEM((HALO + POS, COLS), F32),
            pltpu.VMEM((2, ROWS + 16, SIDE), F32),
            pltpu.VMEM((2, ROWS + 16, SIDE), F32),
            pltpu.VMEM((2, ROWS + 16, SIDE), F32),
            pltpu.VMEM((2, ROWS + 16, SIDE), F32),
            pltpu.VMEM((4, WIDTH, SIDE), F32),
            pltpu.VMEM((2, 2 * WIDTH, SIDE), F32),
            pltpu.VMEM((2, ROWS + 16, SIDE), F32),
            pltpu.VMEM((2, ROWS + 16, SIDE), F32),
            pltpu.VMEM((OWN * SIDE, 2 * SIDE), F32),
            pltpu.SemaphoreType.DMA((SLOTS,)),
            pltpu.SemaphoreType.DMA((SLOTS,)),
            pltpu.SemaphoreType.DMA((8,)),
        ],
        compiler_params=pltpu.CompilerParams(
            collective_id=0, has_side_effects=True, vmem_limit_bytes=60 * 1024 * 1024
        ),
    )(tokens, weights, long_filter, short_filter, skip_gain, *held)
    return out.astype(BF16)


def solution(mesh):
    placed = (P("seq", "ch"), P("seq", None, "ch"), P(None, None, "ch"), P("seq", "ch"), P("ch"))
    return jax.shard_map(
        local, mesh=mesh, in_specs=placed, out_specs=P("seq", "ch"), check_vma=False
    )
```
